256 devices in a mesh: dp: 64 (over z, x_hi, y), mp: 4 (over x_lo, core).
Axes of the slice: x: 4 (x_hi: 2, x_lo: 2; x = x_hi * 2 + x_lo), y: 4, z: 8, core: 2. Of those that a mesh axis runs over, the one named last changes fastest.
Arguments:
- images: bfloat16 [8192, 1152], P('dp'), may hold values from -16 to 16
- captions: bfloat16 [8192, 1152], P('dp'), may hold values from -16 to 16
- image_gain: float32 [1152], replicated, may hold values from 0.5 to 1.5
- fc_in: bfloat16 [1152, 4304], P(None, 'mp'), may hold values from -0.1875 to 0.1875
- fc_out: bfloat16 [4304, 1152], P('mp'), may hold values from -0.09375 to 0.09375
- text_gain: float32 [1152], replicated, may hold values from 0.5 to 1.5
- text_head: bfloat16 [1152, 1152], P(None, 'mp'), may hold values from -2 to 2
- caption_ids: int32 [64, 128], P('dp'), may hold values from 0 to 127, as said below
- logit_scale: float32 [1], replicated, may hold values from 20 to 40
- logit_bias: float32 [1], replicated, may hold values from -12 to -8
Outputs:
- row_loss: float32 [8192], P('dp')
- grad_in: float32 [1152, 4304], P('dp', 'mp')
- grad_out: float32 [4304, 1152], P('mp', 'dp')
- grad_head: float32 [1152, 1152], P('dp', 'mp')
The draws below stay inside these ranges and needn't reach their ends.
Inputs may be any that keep to these rules, and one draw needn't show every extreme that they name: Each row of caption_ids is a permutation of the 128 caption rows of its index of dp.
All inputs are finite; a program needn't handle non-finite values.
Results may differ from the reference program's by a relative error of at most 0.003.
Values may be sent and summed in bfloat16 or wider, within the bound.
A program may use at most 128 MiB of HBM per device.

```python
import math
import jax
import jax.numpy as jnp
from jax import lax

D = 1152
FF = 4304
B_DEV = 128
LOOP = 16
GROUPS = 4
IMAGES = 8192


def shared_parts(key):
    topics = 32
    streams = jax.random.split(key, 4)
    blocks = IMAGES // B_DEV
    centres = jax.random.normal(streams[0], (topics, D), jnp.float32)
    labels = jax.random.randint(streams[1], (blocks, B_DEV), 0, topics)
    ordering = jax.vmap(lambda subkey: jax.random.permutation(subkey, B_DEV))(jax.random.split(streams[2], blocks)).astype(jnp.int32)
    private = jax.random.normal(streams[3], (blocks, B_DEV, D), jnp.float32)
    return (centres, labels, ordering, private)


def blend(key, topic_part, private, low, high, noise):
    strength = jax.random.uniform(key, topic_part.shape[:-1] + (1,), jnp.float32, low, high)
    values = strength * topic_part + 0.7 * private + noise
    return jnp.clip(values, -16.0, 16.0).reshape(IMAGES, D).astype(jnp.bfloat16)


def draw_images(key, part):
    centres, labels, ordering, private = shared_parts(key)
    key = jax.random.fold_in(key, 3)
    noise_key = jax.random.fold_in(key, 1)
    noise = 0.5 * jax.random.normal(noise_key, private.shape, jnp.float32)
    return blend(key, centres[labels], private, 0.15, 0.7, noise)


def draw_captions(key, part):
    centres, labels, ordering, private = shared_parts(key)
    key = jax.random.fold_in(key, 5)
    noise_key = jax.random.fold_in(key, 1)
    inverse = jnp.argsort(ordering, axis=1, stable=True)
    cap_labels = jnp.take_along_axis(labels, inverse, 1)
    cap_private = jnp.take_along_axis(private, jnp.broadcast_to(inverse[:, :, None], private.shape), 1)
    noise = 0.5 * jax.random.normal(noise_key, private.shape, jnp.float32)
    return blend(key, centres[cap_labels], cap_private, 0.15, 0.7, noise)


def draw_caption_ids(key, part):
    centres, labels, ordering, private = shared_parts(key)
    return ordering


def draw_text_head(key, part):
    key = jax.random.fold_in(key, 9)
    diag_key, rest_key = jax.random.split(key)
    identity = (jnp.arange(D)[:, None] == jnp.arange(D)[None, :]).astype(jnp.float32)
    diagonal = jax.random.uniform(diag_key, (D,), jnp.float32, 0.85, 1.15)
    off_diagonal = jax.random.normal(rest_key, (D, D), jnp.float32)
    values = identity * diagonal[None, :] + 0.5 * off_diagonal / math.sqrt(D)
    return jnp.clip(values, -2.0, 2.0).astype(jnp.bfloat16)


def block_levels(key, dims, shards, least, high):
    def one(dim, shards_of):
        heights = jax.random.uniform(jax.random.fold_in(jax.random.fold_in(key, 6), dim), (shards_of,), jnp.float32, least / len(shards), high / len(shards))
        return jnp.repeat(jnp.exp(heights), dims[dim] // shards_of).reshape((-1,) + (1,) * (len(dims) - dim - 1))

    loudness = one(*shards[0])
    for cut in shards[1:]:
        loudness = loudness * one(*cut)
    return loudness


def centred(own_key, extent, scale, most, pieces=(), kind=jnp.bfloat16):
    entries = scale * jax.random.normal(own_key, extent, jnp.float32)
    if pieces:
        entries = entries * block_levels(own_key, extent, pieces, -0.22, 0.18)
    return jnp.clip(entries, -most, most).astype(kind)


def setup_inputs(seed: int = 0) -> dict:
    seeds = jax.random.split(jax.random.key(seed), 11)
    return {
        "images": draw_images(jax.random.fold_in(seeds[10], 71), 0),
        "captions": draw_captions(jax.random.fold_in(seeds[10], 71), 0),
        "image_gain": jnp.clip(1.0 + 0.1 * jax.random.normal(seeds[2], (D,), jnp.float32), 0.5, 1.5),
        "fc_in": centred(seeds[3], (D, FF), D ** -0.5, 0.1875, ((1, 4),)),
        "fc_out": centred(seeds[4], (FF, D), FF ** -0.5, 0.09375, ((0, 4),)),
        "text_gain": jnp.clip(1.0 + 0.1 * jax.random.normal(seeds[5], (D,), jnp.float32), 0.5, 1.5),
        "text_head": draw_text_head(jax.random.fold_in(seeds[10], 71), 0),
        "caption_ids": draw_caption_ids(jax.random.fold_in(seeds[10], 71), 0),
        "logit_scale": jnp.clip(jax.random.uniform(seeds[8], (1,), jnp.float32, 20.0, 40.0), 20.0, 40.0),
        "logit_bias": jnp.clip(jax.random.uniform(seeds[9], (1,), jnp.float32, -12.0, -8.0), -12.0, -8.0),
    }


def layer_norm(values, gain):
    center = values - lax.optimization_barrier(jnp.mean(values, -1, keepdims=True))
    spread = lax.optimization_barrier(jnp.mean(center * center, -1, keepdims=True))
    return center * lax.rsqrt(spread + 1e-06) * gain

def unit_rows(values):
    return values * lax.rsqrt(lax.optimization_barrier(jnp.sum(values * values, -1, keepdims=True)) + 1e-06)

def group_terms(img_group, txt_group, ids_group, scale, bias):
    width = ids_group.shape[1]
    count = ids_group.shape[0] * width
    target = (jnp.arange(ids_group.shape[0], dtype=jnp.int32)[:, None] * width + ids_group).reshape(-1)
    sign = jnp.where(target[:, None] == jnp.arange(count, dtype=jnp.int32)[None, :], 1.0, -1.0).astype(jnp.float32)
    logit = scale * jnp.dot(img_group, txt_group.T, preferred_element_type=jnp.float32) + bias
    loss = lax.optimization_barrier(jnp.sum(jax.nn.softplus(-sign * logit), 1))
    slope = (-sign * jax.nn.sigmoid(-sign * logit) * scale).astype(jnp.bfloat16)
    d_img = jnp.dot(slope, txt_group, preferred_element_type=jnp.float32)
    d_txt = jnp.dot(slope.T, img_group, preferred_element_type=jnp.float32)
    return (loss, d_img, d_txt)

def to_groups(values):
    return values.reshape(LOOP, GROUPS, B_DEV, D).transpose(1, 0, 2, 3).reshape(GROUPS, LOOP * B_DEV, D)

def from_groups(values):
    return values.reshape(GROUPS, LOOP, B_DEV, D).transpose(1, 0, 2, 3).reshape(IMAGES, D)

def reference(images, captions, image_gain, fc_in, fc_out, text_gain, text_head, caption_ids, logit_scale, logit_bias):
    inputs = images.astype(jnp.float32)
    normed = layer_norm(inputs, image_gain).astype(jnp.bfloat16)
    pre = jnp.dot(normed, fc_in, preferred_element_type=jnp.float32)
    act = jax.nn.gelu(pre).astype(jnp.bfloat16)
    feat = inputs + jnp.dot(act, fc_out, preferred_element_type=jnp.float32)
    img_emb = unit_rows(feat).astype(jnp.bfloat16)
    text_normed = layer_norm(captions.astype(jnp.float32), text_gain).astype(jnp.bfloat16)
    head = jnp.dot(text_normed, text_head, preferred_element_type=jnp.float32).astype(jnp.bfloat16)
    head_wide = head.astype(jnp.float32)
    txt_emb = unit_rows(head_wide).astype(jnp.bfloat16)
    scale = logit_scale[0]
    bias = logit_bias[0]
    img_groups = to_groups(img_emb)
    txt_groups = to_groups(txt_emb)
    id_groups = caption_ids.reshape(LOOP, GROUPS, B_DEV).transpose(1, 0, 2)

    def one_group(items):
        return group_terms(items[0], items[1], items[2], scale, bias)
    loss, d_img, d_txt = lax.map(one_group, (img_groups, txt_groups, id_groups))
    row_loss = loss.reshape(GROUPS, LOOP, B_DEV).transpose(1, 0, 2).reshape(-1)
    d_img = from_groups(d_img)
    d_txt = from_groups(d_txt)
    d_feat = jax.vjp(unit_rows, feat)[1](d_img)[0].astype(jnp.bfloat16)
    grad_out = jnp.dot(act.T, d_feat, preferred_element_type=jnp.float32)
    d_act = jnp.dot(d_feat, fc_out.T, preferred_element_type=jnp.float32)
    d_pre = jax.vjp(jax.nn.gelu, pre)[1](d_act)[0].astype(jnp.bfloat16)
    grad_in = jnp.dot(normed.T, d_pre, preferred_element_type=jnp.float32)
    d_head = jax.vjp(unit_rows, head_wide)[1](d_txt)[0].astype(jnp.bfloat16)
    grad_head = jnp.dot(text_normed.T, d_head, preferred_element_type=jnp.float32)
    return (row_loss, grad_in, grad_out, grad_head)
```

```python
import functools
import math

import jax
import jax.numpy as jnp
from jax import lax
from jax.experimental import pallas as pl
from jax.experimental.pallas import tpu as pltpu
from jax.sharding import PartitionSpec as P

NX, NY, NZ = 4, 4, 8
ROWS = 128
QUARTER = 32
D = 1152
HIDDEN = 1076
COLS = 288
OUT = 18
CHUNK = 24
COPIES = 160
F32, BF16 = jnp.float32, jnp.bfloat16
GELU = math.sqrt(2.0 / math.pi)


def dot(left, right):
    return jnp.dot(left, right, preferred_element_type=F32)


def dot_last(left, right):
    return lax.dot_general(left, right, (((1,), (1,)), ((), ())), preferred_element_type=F32)


def layer_norm(values, gain):
    center = values - jnp.mean(values, -1, keepdims=True)
    spread = jnp.mean(center * center, -1, keepdims=True)
    return (center * lax.rsqrt(spread + 1e-06) * gain).astype(BF16)


def unit_scale(values):
    return lax.rsqrt(jnp.sum(values * values, -1, keepdims=True) + 1e-06)


def unit_grad(values, scale, grad):
    inner = jnp.sum(values * grad, -1, keepdims=True)
    return scale * (grad - values * (scale * scale * inner))


def gelu_tanh(pre):
    return jnp.tanh(GELU * (pre + 0.044715 * pre * pre * pre))


def gelu(pre, bend):
    return (0.5 * pre * (1.0 + bend)).astype(BF16)


def gelu_slope(pre, bend):
    return 0.5 * (1.0 + bend) + 0.5 * pre * (1.0 - bend * bend) * (
        GELU * (1.0 + 3.0 * 0.044715 * pre * pre)
    )


def pair_terms(logit, sign, scale):
    arg = -sign * logit
    small = jnp.exp(-jnp.abs(arg))
    loss = jnp.maximum(arg, 0.0) + jnp.log1p(small)
    share = jnp.where(arg >= 0.0, 1.0, small) / (1.0 + small)
    return loss, -sign * share * scale


class Links:
    def __init__(self, send, recv):
        self.send, self.recv, self.started = send, recv, []

    def push(self, src, dst, device):
        at = len(self.started)
        copy = pltpu.make_async_remote_copy(
            src_ref=src,
            dst_ref=dst,
            send_sem=self.send.at[at],
            recv_sem=self.recv.at[at],
            device_id=device,
            device_id_type=pl.DeviceIdType.MESH,
        )
        copy.start()
        self.started.append(copy)
        return copy

    def drain(self):
        for copy in self.started:
            copy.wait_send()


def kernel(
    images,
    captions,
    image_gain,
    fc_in,
    fc_out,
    text_gain,
    text_head,
    ids,
    logit_scale,
    logit_bias,
    loss_out,
    in_out,
    out_out,
    head_out,
    w_in,
    w_out,
    w_head,
    own_images,
    own_captions,
    all_images,
    all_captions,
    all_dfeat,
    all_dhead,
    partial,
    d_img,
    d_txt,
    from_sibling,
    to_across,
    from_across,
    head_parts,
    head_full,
    txt_home,
    img_home,
    txt_units,
    img_units,
    sign_a,
    sign_b,
    matches,
    losses,
    pick_rows,
    pick_cols,
    act_all,
    slope_all,
    normed_t,
    text_t,
    grad_in,
    grad_out,
    grad_head,
    land_in,
    land_out,
    land_head,
    send_sems,
    recv_sems,
    load_sems,
):
    dp, mp = lax.axis_index("dp"), lax.axis_index("mp")
    z, xh, y = dp // 8, (dp // 4) % 2, dp % 4
    xl, c = mp // 2, mp % 2
    x = 2 * xh + xl
    x_lo, x_far, x_pn = 2 * xh + (1 - xl), 2 * (1 - xh) + xl, 3 - x

    def place(z_, xh_, y_, xl_, c_):
        return {"dp": z_ * 8 + xh_ * 4 + y_, "mp": xl_ * 2 + c_}

    sibling = place(z, xh, y, xl, 1 - c)
    across = place(z, xh, y, 1 - xl, c)
    diagonal = place(z, xh, y, 1 - xl, 1 - c)
    partner = place(z, 1 - xh, y, 1 - xl, c)
    y_up, y_down = place(z, xh, (y + 1) % 4, xl, c), place(z, xh, (y + 3) % 4, xl, c)
    z_up, z_down = place((z + 1) % 8, xh, y, xl, c), place((z + 7) % 8, xh, y, xl, c)

    own_slot = (x * 2 + c) * 4 + y
    loads = [
        pltpu.make_async_copy(images, own_images, load_sems.at[0]),
        pltpu.make_async_copy(captions, own_captions, load_sems.at[1]),
        pltpu.make_async_copy(images.at[mp], all_images.at[own_slot], load_sems.at[2]),
        pltpu.make_async_copy(captions.at[mp], all_captions.at[own_slot], load_sems.at[3]),
        pltpu.make_async_copy(text_head, w_head, load_sems.at[4]),
        pltpu.make_async_copy(fc_in, w_in, load_sems.at[5]),
        pltpu.make_async_copy(fc_out, w_out, load_sems.at[6]),
    ]
    for load in loads:
        load.start()

    barrier = pltpu.get_barrier_semaphore()
    peers = (sibling, across, diagonal, partner, y_up, y_down, z_up, z_down)
    for peer in peers:
        pl.semaphore_signal(barrier, inc=1, device_id=peer, device_id_type=pl.DeviceIdType.MESH)

    pos = xh * 4 + y
    row = lax.broadcasted_iota(jnp.int32, (NZ * CHUNK, D), 0)
    col = lax.broadcasted_iota(jnp.int32, (NZ * CHUNK, D), 1)
    chunk, inside = row // CHUNK, row % CHUNK
    picked = (col == chunk * (8 * OUT) + pos * OUT + inside) & (inside < OUT)
    pick_rows[...] = jnp.where(picked, 1.0, 0.0).astype(BF16)
    row = lax.broadcasted_iota(jnp.int32, (D, COLS), 0)
    col = lax.broadcasted_iota(jnp.int32, (D, COLS), 1)
    pick_cols[...] = jnp.where(row == mp * COLS + col, 1.0, 0.0).astype(BF16)

    caption = lax.broadcasted_iota(jnp.int32, (ROWS, ROWS), 0)
    match = jnp.where(caption == ids[...], 1.0, -1.0).astype(F32)
    sign_a[...] = jnp.full(sign_a.shape, -1.0, F32)
    sign_b[...] = jnp.full(sign_b.shape, -1.0, F32)
    head_full[...] = jnp.zeros(head_full.shape, F32)
    matches[...] = match.reshape(matches.shape)
    sign_a[z * 2] = matches[mp]
    matches[...] = match.T.reshape(matches.shape)
    sign_b[z * 2] = matches[mp]

    scale, bias = logit_scale[0], logit_bias[0]
    links = Links(send_sems, recv_sems)
    push = links.push
    pl.semaphore_wait(barrier, len(peers))

    class PlaneGather:
        def __init__(self, buf):
            self.buf = buf

        def column(self, x_, part=None):
            first = (x_ * 2 + c) * 4
            if part is None:
                return self.buf.at[pl.ds(first, 4)]
            return self.buf.at[pl.ds(first + 2 * part, 2)]

        def y1(self):
            own = self.buf.at[own_slot]
            self.up = push(own, own, y_up)
            self.down = push(own, own, y_down)

        def y2(self):
            first = (x * 2 + c) * 4
            self.up.wait_recv()
            half = self.buf.at[first + (y + 3) % 4, pl.ds(0, 16)]
            self.up2 = push(half, half, y_up)
            self.down.wait_recv()
            half = self.buf.at[first + (y + 1) % 4, pl.ds(16, 16)]
            self.down2 = push(half, half, y_down)

        def x1(self):
            self.up2.wait_recv()
            self.down2.wait_recv()
            own = self.column(x)
            self.sib = push(own, own, sibling)
            self.lo = push(own, own, across)
            self.pn = push(own, own, partner)

        def x2(self):
            self.lo.wait_recv()
            part = self.column(x_lo, 0)
            self.pn2 = push(part, part, partner)
            whole = self.column(x_lo)
            self.sib_lo = push(whole, whole, sibling)
            self.pn.wait_recv()
            part = self.column(x_pn, 1)
            self.lo2 = push(part, part, across)
            whole = self.column(x_pn)
            self.sib_pn = push(whole, whole, sibling)

        def x3(self):
            self.lo2.wait_recv()
            self.pn2.wait_recv()
            whole = self.column(x_far)
            self.sib_far = push(whole, whole, sibling)

        def ready(self, which):
            getattr(self, ("sib", "sib_lo", "sib_pn", "sib_far")[which]).wait_recv()

    block_x = (x, x_lo, x_pn, x_far)

    class QuadSum:
        def __init__(self, buf, at):
            self.buf, self.at = buf, at

        def s1(self):
            self.first = [
                push(self.buf.at[1 - c], from_sibling.at[self.at, 0], sibling),
                push(self.buf.at[2 + 1 - c], from_sibling.at[self.at, 1], sibling),
            ]

        def s2(self):
            for copy in self.first:
                copy.wait_recv()
            to_across[self.at] = self.buf[(1 - xl) * 2 + c] + from_sibling[self.at, 1 - xl]
            self.second = push(to_across.at[self.at], from_across.at[self.at], across)

        def total(self):
            mine = self.buf[mp] + from_sibling[self.at, xl]
            self.second.wait_recv()
            return mine + from_across[self.at]

    for load in loads[:4]:
        load.wait()
    images_plane, captions_plane = PlaneGather(all_images), PlaneGather(all_captions)
    images_plane.y1()
    captions_plane.y1()

    values = own_captions[...].reshape(ROWS, D).astype(F32)
    text_normed = layer_norm(values, text_gain[...])
    loads[4].wait()
    head_parts[mp] = dot(text_normed, w_head[...]).astype(BF16)
    head_copies = [
        push(head_parts.at[mp], head_parts.at[mp], peer) for peer in (sibling, across, diagonal)
    ]

    values = own_images[...].reshape(ROWS, D).astype(F32)
    normed = layer_norm(values, image_gain[...])
    loads[5].wait()
    pre = dot(normed, w_in[...])
    act = gelu(pre, gelu_tanh(pre))
    loads[6].wait()
    partial[...] = dot(act, w_out[...]).reshape(partial.shape)
    feat_sum = QuadSum(partial, 0)
    feat_sum.s1()
    images_plane.y2()
    captions_plane.y2()
    feat_sum.s2()

    for copy in head_copies:
        copy.wait_recv()
    for part in range(4):
        row = lax.broadcasted_iota(jnp.int32, (COLS, D), 0)
        col = lax.broadcasted_iota(jnp.int32, (COLS, D), 1)
        spread = jnp.where(col == part * COLS + row, 1.0, 0.0).astype(BF16)
        head_full[...] += dot(head_parts[part], spread).reshape(head_full.shape)
    head = head_full[...].reshape(ROWS, D)
    txt_home[...] = (head * unit_scale(head)).astype(BF16).reshape(txt_home.shape)
    txt_units[z, 0] = txt_home[mp]

    class TextRing:
        def unit(self, z_, half=None):
            slot = txt_units.at[z_ % 8, 0]
            return slot if half is None else slot.at[pl.ds(16 * half, 16)]

        def share(self, z_):
            self.shared.append(push(txt_units.at[z_ % 8, 0], txt_units.at[z_ % 8, 1], partner))

        def start(self):
            self.shared = []
            self.up = push(self.unit(z), self.unit(z), z_up)
            self.down = push(self.unit(z), self.unit(z), z_down)
            self.share(z)

        def step(self, at):
            half = at == 3
            self.up.wait_recv()
            unit = self.unit(z + 8 - at, 0 if half else None)
            self.up = push(unit, unit, z_up)
            self.share(z + 8 - at)
            self.down.wait_recv()
            unit = self.unit(z + at, 1 if half else None)
            self.down = push(unit, unit, z_down)
            self.share(z + at)

        def finish(self):
            self.up.wait_recv()
            self.down.wait_recv()
            self.share(z + 4)
            for copy in self.shared:
                copy.wait_recv()

    text_ring = TextRing()
    text_ring.start()

    feat = own_images[mp].astype(F32) + feat_sum.total()
    feat_scale = unit_scale(feat)
    img_home[mp] = (feat * feat_scale).astype(BF16)
    img_units[z, 0] = img_home[mp]
    img_partner = push(img_units.at[z, 0], img_units.at[z, 1], partner)
    img_copies = [push(img_home.at[mp], img_home.at[mp], peer) for peer in (sibling, across, diagonal)]

    class ImageRing:
        def unit(self, z_, half=None):
            return img_units.at[z_ % 8] if half is None else img_units.at[z_ % 8, half]

        def start(self):
            img_partner.wait_recv()
            self.up = push(self.unit(z), self.unit(z), z_up)
            self.down = push(self.unit(z), self.unit(z), z_down)

        def step(self, at):
            half = at == 3
            self.up.wait_recv()
            unit = self.unit(z + 8 - at, 0 if half else None)
            self.up = push(unit, unit, z_up)
            self.down.wait_recv()
            unit = self.unit(z + at, 1 if half else None)
            self.down = push(unit, unit, z_down)

        def finish(self):
            self.up.wait_recv()
            self.down.wait_recv()

    image_ring = ImageRing()
    images_plane.x1()
    image_ring.start()
    text_ring.step(1)
    captions_plane.x1()
    text_ring.step(2)
    image_ring.step(1)
    text_ring.step(3)
    images_plane.x2()
    image_ring.step(2)
    for copy in img_copies:
        copy.wait_recv()
    text_ring.finish()

    img_rows = img_home[...].reshape(ROWS, D)
    units = txt_units[...].reshape(16 * QUARTER, D)
    logit = scale * dot_last(units, img_rows) + bias
    loss, slope = pair_terms(logit, sign_a[...].reshape(16 * QUARTER, ROWS), scale)
    losses[mp] = jnp.broadcast_to(jnp.sum(loss, 0, keepdims=True), losses.shape[1:])
    loss_copies = [push(losses.at[mp], losses.at[mp], peer) for peer in (sibling, across, diagonal)]
    d_img[...] = dot(slope.T.astype(BF16), units).reshape(d_img.shape)
    img_sum = QuadSum(d_img, 1)
    img_sum.s1()
    image_ring.step(3)
    captions_plane.x2()
    images_plane.x3()
    img_sum.s2()
    captions_plane.x3()
    grad = unit_grad(feat, feat_scale, img_sum.total())
    all_dfeat[own_slot] = grad.astype(BF16)
    dfeat_plane = PlaneGather(all_dfeat)
    dfeat_plane.y1()

    image_ring.finish()
    txt_rows = txt_home[...].reshape(ROWS, D)
    units = img_units[...].reshape(16 * QUARTER, D)
    logit = scale * dot_last(units, txt_rows) + bias
    _, slope = pair_terms(logit, sign_b[...].reshape(16 * QUARTER, ROWS), scale)
    d_txt[...] = dot(slope.T.astype(BF16), units).reshape(d_txt.shape)
    txt_sum = QuadSum(d_txt, 2)
    txt_sum.s1()
    dfeat_plane.y2()
    txt_sum.s2()
    dfeat_plane.x1()
    head = head_full[mp]
    grad = unit_grad(head, unit_scale(head), txt_sum.total())
    all_dhead[own_slot] = grad.astype(BF16)
    dhead_plane = PlaneGather(all_dhead)
    dhead_plane.y1()

    def forward_block(at, carry):
        values = all_images[pl.ds(at * 8, 8)].reshape(256, D).astype(F32)
        normed = layer_norm(values, image_gain[...])
        normed_t[at] = dot_last(pick_rows[...], normed).astype(BF16)
        pre = dot(normed, w_in[...])
        bend = gelu_tanh(pre)
        act_all[at] = gelu(pre, bend)
        slope_all[at] = gelu_slope(pre, bend)
        values = all_captions[pl.ds(at * 8, 8)].reshape(256, D).astype(F32)
        text_t[at] = dot_last(pick_rows[...], layer_norm(values, text_gain[...])).astype(BF16)
        return carry

    for which in range(4):
        images_plane.ready(which)
        captions_plane.ready(which)
    lax.fori_loop(0, 4, forward_block, 0)
    dfeat_plane.x2()
    dhead_plane.y2()

    grad_in[...] = jnp.zeros(grad_in.shape, F32)
    grad_out[...] = jnp.zeros(grad_out.shape, F32)
    grad_head[...] = jnp.zeros(grad_head.shape, F32)

    def backward_block(at):
        d_feat = all_dfeat[pl.ds(at * 8, 8)].reshape(256, D)
        d_pre = (dot_last(d_feat, w_out[...]) * slope_all[at]).astype(BF16)
        d_feat_t = dot_last(pick_rows[...], d_feat).astype(BF16)
        grad_in[...] += dot(normed_t[at], d_pre).reshape(grad_in.shape)
        grad_out[...] += dot(d_feat_t, act_all[at]).reshape(grad_out.shape)

    def head_block(at, carry):
        d_head = all_dhead[pl.ds(at * 8, 8)].reshape(256, D)
        d_cols = dot(d_head, pick_cols[...]).astype(BF16)
        grad_head[...] += dot(text_t[at], d_cols).reshape(grad_head.shape)
        return carry

    dfeat_plane.ready(0)
    backward_block(block_x[0])
    dfeat_plane.x3()
    dhead_plane.x1()
    for which in range(1, 4):
        dfeat_plane.ready(which)
        backward_block(block_x[which])

    class RingSum:
        def __init__(self, buf, land, far_up):
            self.buf, self.land = buf, land
            self.first = (1, 2) if far_up else (2, 1)
            self.copy = [None, None]

        def step(self, at):
            for way in range(2):
                if at < self.first[way]:
                    continue
                dest = (z + 5 - at) % 8 if way == 0 else (z + 3 + at) % 8
                if at > self.first[way]:
                    self.copy[way].wait_recv()
                    self.buf[dest] += self.land[way, at - 2]
                self.copy[way] = push(
                    self.buf.at[dest], self.land.at[way, at - 1], (z_up, z_down)[way]
                )

        def total(self):
            for way in range(2):
                self.copy[way].wait_recv()
            return self.buf[z] + self.land[0, 3] + self.land[1, 3]

    ring_in, ring_out = RingSum(grad_in, land_in, True), RingSum(grad_out, land_out, False)
    ring_head = RingSum(grad_head, land_head, True)
    ring_in.step(1)
    ring_out.step(1)
    dhead_plane.x2()
    ring_in.step(2)
    ring_out.step(2)
    dhead_plane.x3()
    for which in range(4):
        dhead_plane.ready(which)
    lax.fori_loop(0, 4, head_block, 0)
    ring_head.step(1)
    ring_in.step(3)
    ring_out.step(3)
    ring_head.step(2)
    ring_in.step(4)
    ring_out.step(4)
    ring_head.step(3)
    ring_head.step(4)
    for copy in loss_copies:
        copy.wait_recv()
    loss_out[...] = ((losses[0] + losses[1]) + (losses[2] + losses[3]))[:1]
    in_out[...] = ring_in.total()[:OUT]
    out_out[...] = ring_out.total()[:OUT]
    head_out[...] = ring_head.total()[:OUT]
    links.drain()


def on_device(
    images,
    captions,
    image_gain,
    fc_in,
    fc_out,
    text_gain,
    text_head,
    caption_ids,
    logit_scale,
    logit_bias,
):
    whole = pl.BlockSpec(memory_space=pltpu.VMEM)
    far = pl.BlockSpec(memory_space=pl.ANY)
    scalar = pl.BlockSpec(memory_space=pltpu.SMEM)
    vmem = pltpu.VMEM
    loss, grad_in, grad_out, grad_head = pl.pallas_call(
        kernel,
        out_shape=(
            jax.ShapeDtypeStruct((1, ROWS), F32),
            jax.ShapeDtypeStruct((OUT, HIDDEN), F32),
            jax.ShapeDtypeStruct((OUT, HIDDEN), F32),
            jax.ShapeDtypeStruct((OUT, COLS), F32),
        ),
        in_specs=[far, far, whole, far, far, whole, far, whole, scalar, scalar],
        out_specs=(whole, whole, whole, whole),
        scratch_shapes=[
            vmem((D, HIDDEN), BF16),
            vmem((HIDDEN, D), BF16),
            vmem((D, COLS), BF16),
            vmem((4, QUARTER, D), BF16),
            vmem((4, QUARTER, D), BF16),
            vmem((32, QUARTER, D), BF16),
            vmem((32, QUARTER, D), BF16),
            vmem((32, QUARTER, D), BF16),
            vmem((32, QUARTER, D), BF16),
            vmem((4, QUARTER, D), F32),
            vmem((4, QUARTER, D), F32),
            vmem((4, QUARTER, D), F32),
            vmem((3, 2, QUARTER, D), F32),
            vmem((3, QUARTER, D), F32),
            vmem((3, QUARTER, D), F32),
            vmem((4, ROWS, COLS), BF16),
            vmem((4, QUARTER, D), F32),
            vmem((4, QUARTER, D), BF16),
            vmem((4, QUARTER, D), BF16),
            vmem((NZ, 2, QUARTER, D), BF16),
            vmem((NZ, 2, QUARTER, D), BF16),
            vmem((16, QUARTER, ROWS), F32),
            vmem((16, QUARTER, ROWS), F32),
            vmem((4, QUARTER, ROWS), F32),
            vmem((4, 8, ROWS), F32),
            vmem((NZ * CHUNK, D), BF16),
            vmem((D, COLS), BF16),
            vmem((4, 256, HIDDEN), BF16),
            vmem((4, 256, HIDDEN), F32),
            vmem((4, NZ * CHUNK, 256), BF16),
            vmem((4, NZ * CHUNK, 256), BF16),
            vmem((NZ, CHUNK, HIDDEN), F32),
            vmem((NZ, CHUNK, HIDDEN), F32),
            vmem((NZ, CHUNK, COLS), F32),
            vmem((2, 4, CHUNK, HIDDEN), F32),
            vmem((2, 4, CHUNK, HIDDEN), F32),
            vmem((2, 4, CHUNK, COLS), F32),
            pltpu.SemaphoreType.DMA((COPIES,)),
            pltpu.SemaphoreType.DMA((COPIES,)),
            pltpu.SemaphoreType.DMA((7,)),
        ],
        compiler_params=pltpu.CompilerParams(
            collective_id=0, has_side_effects=True, vmem_limit_bytes=56 * 1024 * 1024
        ),
        name="window",
    )(
        images.reshape(4, QUARTER, D),
        captions.reshape(4, QUARTER, D),
        image_gain.reshape(1, D),
        fc_in,
        fc_out,
        text_gain.reshape(1, D),
        text_head,
        caption_ids,
        logit_scale,
        logit_bias,
    )
    return loss.reshape(ROWS), grad_in, grad_out.T, grad_head


def solution(mesh):
    placed = (
        P("dp", None),
        P("dp", None),
        P(),
        P(None, "mp"),
        P("mp", None),
        P(),
        P(None, "mp"),
        P("dp", None),
        P(),
        P(),
    )
    return jax.shard_map(
        on_device,
        mesh=mesh,
        in_specs=placed,
        out_specs=(P("dp"), P("dp", "mp"), P("mp", "dp"), P("dp", "mp")),
        check_vma=False,
    )
```

```python
import functools
import math

import jax
import jax.numpy as jnp
from jax import lax
from jax.experimental import pallas as pl
from jax.experimental.pallas import tpu as pltpu
from jax.sharding import PartitionSpec as P

NX, NY, NZ = 4, 4, 8
ROWS = 128
QUARTER = 32
D = 1152
HIDDEN = 1076
COLS = 288
OUT = 18
CHUNK = 24
HEAD_CHUNK = 32
COPIES = 160
F32, BF16 = jnp.float32, jnp.bfloat16
GELU = math.sqrt(2.0 / math.pi)


def dot(left, right):
    return jnp.dot(left, right, preferred_element_type=F32)


def dot_last(left, right):
    return lax.dot_general(left, right, (((1,), (1,)), ((), ())), preferred_element_type=F32)


def layer_norm(values, gain):
    center = values - jnp.mean(values, -1, keepdims=True)
    spread = jnp.mean(center * center, -1, keepdims=True)
    return (center * lax.rsqrt(spread + 1e-06) * gain).astype(BF16)


def unit_scale(values):
    return lax.rsqrt(jnp.sum(values * values, -1, keepdims=True) + 1e-06)


def unit_grad(values, scale, grad):
    inner = jnp.sum(values * grad, -1, keepdims=True)
    return scale * (grad - values * (scale * scale * inner))


def gelu_tanh(pre):
    return jnp.tanh(GELU * (pre + 0.044715 * pre * pre * pre))


def gelu(pre, bend):
    return (0.5 * pre * (1.0 + bend)).astype(BF16)


def gelu_slope(pre, bend):
    return 0.5 * (1.0 + bend) + 0.5 * pre * (1.0 - bend * bend) * (
        GELU * (1.0 + 3.0 * 0.044715 * pre * pre)
    )


def pair_terms(logit, sign, scale):
    arg = -sign * logit
    small = jnp.exp(-jnp.abs(arg))
    loss = jnp.maximum(arg, 0.0) + jnp.log1p(small)
    share = jnp.where(arg >= 0.0, 1.0, small) / (1.0 + small)
    return loss, -sign * share * scale


class Links:
    def __init__(self, send, recv):
        self.send, self.recv, self.started = send, recv, []

    def push(self, src, dst, device):
        at = len(self.started)
        copy = pltpu.make_async_remote_copy(
            src_ref=src,
            dst_ref=dst,
            send_sem=self.send.at[at],
            recv_sem=self.recv.at[at],
            device_id=device,
            device_id_type=pl.DeviceIdType.MESH,
        )
        copy.start()
        self.started.append(copy)
        return copy

    def drain(self):
        for copy in self.started:
            copy.wait_send()


def kernel(
    images,
    captions,
    image_gain,
    fc_in,
    fc_out,
    text_gain,
    text_head,
    ids,
    logit_scale,
    logit_bias,
    loss_out,
    in_out,
    out_out,
    head_out,
    w_in,
    w_out,
    w_head,
    own_images,
    own_captions,
    all_images,
    all_captions,
    all_dfeat,
    all_dhead,
    partial,
    d_img,
    d_txt,
    from_sibling,
    to_across,
    from_across,
    head_parts,
    head_full,
    txt_home,
    img_home,
    txt_units,
    img_units,
    sign_a,
    sign_b,
    matches,
    losses,
    pick_rows,
    pick_cols,
    act_all,
    slope_all,
    normed_t,
    text_t,
    grad_in,
    grad_out,
    grad_head,
    packed,
    stage_main,
    stage_head,
    land_main,
    land_head,
    send_sems,
    recv_sems,
    load_sems,
):
    dp, mp = lax.axis_index("dp"), lax.axis_index("mp")
    z, xh, y = dp // 8, (dp // 4) % 2, dp % 4
    xl, c = mp // 2, mp % 2
    x = 2 * xh + xl
    x_lo, x_pn = 2 * xh + (1 - xl), 3 - x
    y_above, y_below, y_far = (y + 1) % 4, (y + 3) % 4, (y + 2) % 4

    def place(z_, xh_, y_, xl_, c_):
        return {"dp": z_ * 8 + xh_ * 4 + y_, "mp": xl_ * 2 + c_}

    sibling = place(z, xh, y, xl, 1 - c)
    across = place(z, xh, y, 1 - xl, c)
    diagonal = place(z, xh, y, 1 - xl, 1 - c)
    partner = place(z, 1 - xh, y, 1 - xl, c)
    y_up, y_down = place(z, xh, y_above, xl, c), place(z, xh, y_below, xl, c)
    z_up, z_down = place((z + 1) % 8, xh, y, xl, c), place((z + 7) % 8, xh, y, xl, c)

    own_slot = (y * 2 + c) * 4 + x
    loads = [
        pltpu.make_async_copy(images, own_images, load_sems.at[0]),
        pltpu.make_async_copy(captions, own_captions, load_sems.at[1]),
        pltpu.make_async_copy(images.at[mp], all_images.at[own_slot], load_sems.at[2]),
        pltpu.make_async_copy(captions.at[mp], all_captions.at[own_slot], load_sems.at[3]),
        pltpu.make_async_copy(text_head, w_head, load_sems.at[4]),
        pltpu.make_async_copy(fc_in, w_in, load_sems.at[5]),
        pltpu.make_async_copy(fc_out, w_out, load_sems.at[6]),
    ]
    for load in loads:
        load.start()

    barrier = pltpu.get_barrier_semaphore()
    peers = (sibling, across, diagonal, partner, y_up, y_down, z_up, z_down)
    for peer in peers:
        pl.semaphore_signal(barrier, inc=1, device_id=peer, device_id_type=pl.DeviceIdType.MESH)

    scale, bias = logit_scale[0], logit_bias[0]
    links = Links(send_sems, recv_sems)
    push = links.push
    pl.semaphore_wait(barrier, len(peers))

    class PlaneGather:
        def __init__(self, buf):
            self.buf = buf

        def group(self, y_, part=None):
            first = (y_ * 2 + c) * 4
            if part is None:
                return self.buf.at[pl.ds(first, 4)]
            return self.buf.at[pl.ds(first + 2 * part, 2)]

        def x1(self):
            own = self.buf.at[own_slot]
            self.lo = push(own, own, across)
            self.pn = push(own, own, partner)

        def x2(self):
            first = (y * 2 + c) * 4
            self.lo.wait_recv()
            half = self.buf.at[first + x_lo, pl.ds(0, 16)]
            self.pn2 = push(half, half, partner)
            self.pn.wait_recv()
            half = self.buf.at[first + x_pn, pl.ds(16, 16)]
            self.lo2 = push(half, half, across)

        def y1(self):
            self.pn2.wait_recv()
            self.lo2.wait_recv()
            own = self.group(y)
            self.sib = push(own, own, sibling)
            self.up = push(own, own, y_up)
            self.down = push(own, own, y_down)

        def y2(self):
            self.up.wait_recv()
            part = self.group(y_below, 0)
            self.up2 = push(part, part, y_up)
            whole = self.group(y_below)
            self.sib_up = push(whole, whole, sibling)
            self.down.wait_recv()
            part = self.group(y_above, 1)
            self.down2 = push(part, part, y_down)
            whole = self.group(y_above)
            self.sib_down = push(whole, whole, sibling)

        def y3(self):
            self.up2.wait_recv()
            self.down2.wait_recv()
            whole = self.group(y_far)
            self.sib_far = push(whole, whole, sibling)

        def ready(self, which):
            getattr(self, ("sib", "sib_up", "sib_down", "sib_far")[which]).wait_recv()

    blocks = (y, y_below, y_above, y_far)

    class QuadSum:
        def __init__(self, buf, at):
            self.buf, self.at = buf, at

        def s1(self):
            self.first = [
                push(self.buf.at[1 - c], from_sibling.at[self.at, 0], sibling),
                push(self.buf.at[2 + 1 - c], from_sibling.at[self.at, 1], sibling),
            ]

        def s2(self):
            for copy in self.first:
                copy.wait_recv()
            to_across[self.at] = self.buf[(1 - xl) * 2 + c] + from_sibling[self.at, 1 - xl]
            self.second = push(to_across.at[self.at], from_across.at[self.at], across)

        def total(self):
            mine = self.buf[mp] + from_sibling[self.at, xl]
            self.second.wait_recv()
            return mine + from_across[self.at]

    for load in loads[:4]:
        load.wait()
    images_plane, captions_plane = PlaneGather(all_images), PlaneGather(all_captions)
    images_plane.x1()
    captions_plane.x1()

    values = own_captions[...].reshape(ROWS, D).astype(F32)
    text_normed = layer_norm(values, text_gain[...].reshape(1, D))
    loads[4].wait()
    head_parts[mp] = dot_last(text_normed, w_head[...]).astype(BF16)
    head_copies = [
        push(head_parts.at[mp], head_parts.at[mp], peer) for peer in (sibling, across, diagonal)
    ]

    images_plane.x2()
    captions_plane.x2()

    values = own_images[...].reshape(ROWS, D).astype(F32)
    normed = layer_norm(values, image_gain[...].reshape(1, D))
    loads[5].wait()
    pre = dot_last(normed, w_in[...])
    act = gelu(pre, gelu_tanh(pre))
    loads[6].wait()
    partial[...] = dot(act, w_out[...]).reshape(partial.shape)
    feat_sum = QuadSum(partial, 0)
    feat_sum.s1()
    images_plane.y1()
    captions_plane.y1()

    chunk = lax.broadcasted_iota(jnp.int32, (NZ, CHUNK, D), 0)
    inside = lax.broadcasted_iota(jnp.int32, (NZ, CHUNK, D), 1)
    col = lax.broadcasted_iota(jnp.int32, (NZ, CHUNK, D), 2)
    pos = xh * 4 + y
    picked = (col == chunk * (8 * OUT) + pos * OUT + inside) & (inside < OUT)
    pick_rows[...] = jnp.where(picked, 1.0, 0.0).reshape(NZ * CHUNK, D).astype(BF16)
    row = lax.broadcasted_iota(jnp.int32, (D, COLS), 0)
    col = lax.broadcasted_iota(jnp.int32, (D, COLS), 1)
    pick_cols[...] = jnp.where(row == mp * COLS + col, 1.0, 0.0).astype(BF16)

    caption = lax.broadcasted_iota(jnp.int32, (ROWS, ROWS), 0)
    match = jnp.where(caption == ids[...], 1.0, -1.0).astype(F32)
    sign_a[...] = jnp.full(sign_a.shape, -1.0, F32)
    sign_b[...] = jnp.full(sign_b.shape, -1.0, F32)
    matches[...] = match.reshape(matches.shape)
    sign_a[z * 2] = matches[mp]
    matches[...] = match.T.reshape(matches.shape)
    sign_b[z * 2] = matches[mp]
    grad_in[...] = jnp.zeros(grad_in.shape, F32)
    grad_out[...] = jnp.zeros(grad_out.shape, F32)
    grad_head[...] = jnp.zeros(grad_head.shape, F32)
    packed[...] = jnp.zeros(packed.shape, F32)

    feat_sum.s2()

    for copy in head_copies:
        copy.wait_recv()
    head = jnp.concatenate([head_parts[part].astype(F32) for part in range(4)], 1)
    head_full[...] = head.reshape(head_full.shape)
    txt_home[...] = (head * unit_scale(head)).astype(BF16).reshape(txt_home.shape)
    txt_units[z, 0] = txt_home[mp]

    class TextRing:
        def unit(self, z_, half=None):
            slot = txt_units.at[z_ % 8, 0]
            return slot if half is None else slot.at[pl.ds(16 * half, 16)]

        def share(self, z_):
            self.shared.append(push(txt_units.at[z_ % 8, 0], txt_units.at[z_ % 8, 1], partner))

        def start(self):
            self.shared = []
            self.up = push(self.unit(z), self.unit(z), z_up)
            self.down = push(self.unit(z), self.unit(z), z_down)
            self.share(z)

        def step(self, at):
            half = at == 3
            self.up.wait_recv()
            unit = self.unit(z + 8 - at, 0 if half else None)
            self.up = push(unit, unit, z_up)
            self.share(z + 8 - at)
            self.down.wait_recv()
            unit = self.unit(z + at, 1 if half else None)
            self.down = push(unit, unit, z_down)
            self.share(z + at)

        def finish(self):
            self.up.wait_recv()
            self.down.wait_recv()
            self.share(z + 4)
            for copy in self.shared:
                copy.wait_recv()

    text_ring = TextRing()
    text_ring.start()

    feat = own_images[mp].astype(F32) + feat_sum.total()
    feat_scale = unit_scale(feat)
    img_home[mp] = (feat * feat_scale).astype(BF16)
    img_units[z, 0] = img_home[mp]
    img_partner = push(img_units.at[z, 0], img_units.at[z, 1], partner)
    img_copies = [push(img_home.at[mp], img_home.at[mp], peer) for peer in (sibling, across, diagonal)]

    class ImageRing:
        def unit(self, z_, half=None):
            return img_units.at[z_ % 8] if half is None else img_units.at[z_ % 8, half]

        def start(self):
            img_partner.wait_recv()
            self.up = push(self.unit(z), self.unit(z), z_up)
            self.down = push(self.unit(z), self.unit(z), z_down)

        def step(self, at):
            half = at == 3
            self.up.wait_recv()
            unit = self.unit(z + 8 - at, 0 if half else None)
            self.up = push(unit, unit, z_up)
            self.down.wait_recv()
            unit = self.unit(z + at, 1 if half else None)
            self.down = push(unit, unit, z_down)

        def finish(self):
            self.up.wait_recv()
            self.down.wait_recv()

    def forward_block(which):
        at = blocks[which]
        images_plane.ready(which)
        values = all_images[pl.ds(at * 8, 8)].reshape(256, D).astype(F32)
        normed = layer_norm(values, image_gain[...].reshape(1, D))
        normed_t[at] = dot_last(pick_rows[...], normed).astype(BF16)
        pre = dot_last(normed, w_in[...])
        bend = gelu_tanh(pre)
        act_all[at] = gelu(pre, bend)
        slope_all[at] = gelu_slope(pre, bend)
        captions_plane.ready(which)
        values = all_captions[pl.ds(at * 8, 8)].reshape(256, D).astype(F32)
        text_normed = layer_norm(values, text_gain[...].reshape(1, D))
        text_t[at] = dot_last(pick_rows[...], text_normed).astype(BF16)

    image_ring = ImageRing()
    image_ring.start()
    text_ring.step(1)
    images_plane.y2()
    captions_plane.y2()
    forward_block(0)
    text_ring.step(2)
    image_ring.step(1)
    forward_block(1)
    text_ring.step(3)
    image_ring.step(2)
    images_plane.y3()
    captions_plane.y3()
    forward_block(2)
    for copy in img_copies:
        copy.wait_recv()
    text_ring.finish()

    img_rows = img_home[...].reshape(ROWS, D)
    units = txt_units[...].reshape(16 * QUARTER, D)
    logit = scale * dot_last(units, img_rows) + bias
    loss, slope = pair_terms(logit, sign_a[...].reshape(16 * QUARTER, ROWS), scale)
    losses[mp] = jnp.broadcast_to(jnp.sum(loss, 0, keepdims=True), losses.shape[1:])
    loss_copies = [push(losses.at[mp], losses.at[mp], peer) for peer in (sibling, across, diagonal)]
    d_img[...] = dot(slope.T.astype(BF16), units).reshape(d_img.shape)
    img_sum = QuadSum(d_img, 1)
    img_sum.s1()
    image_ring.step(3)
    img_sum.s2()
    forward_block(3)
    grad = unit_grad(feat, feat_scale, img_sum.total())
    all_dfeat[own_slot] = grad.astype(BF16)
    dfeat_plane = PlaneGather(all_dfeat)
    dfeat_plane.x1()

    image_ring.finish()
    txt_rows = txt_home[...].reshape(ROWS, D)
    units = img_units[...].reshape(16 * QUARTER, D)
    logit = scale * dot_last(units, txt_rows) + bias
    _, slope = pair_terms(logit, sign_b[...].reshape(16 * QUARTER, ROWS), scale)
    d_txt[...] = dot(slope.T.astype(BF16), units).reshape(d_txt.shape)
    txt_sum = QuadSum(d_txt, 2)
    txt_sum.s1()
    dfeat_plane.x2()
    txt_sum.s2()
    dfeat_plane.y1()
    head = head_full[mp]
    grad = unit_grad(head, unit_scale(head), txt_sum.total())
    all_dhead[own_slot] = grad.astype(BF16)
    dhead_plane = PlaneGather(all_dhead)
    dhead_plane.x1()

    def backward_block(at):
        d_feat = all_dfeat[pl.ds(at * 8, 8)].reshape(256, D)
        d_pre = (dot_last(d_feat, w_out[...]) * slope_all[at]).astype(BF16)
        d_feat_t = dot_last(pick_rows[...], d_feat).astype(BF16)
        grad_in[...] += dot(normed_t[at], d_pre).reshape(grad_in.shape)
        grad_out[...] += dot(d_feat_t, act_all[at]).reshape(grad_out.shape)

    def head_block(at):
        d_head = all_dhead[pl.ds(at * 8, 8)].reshape(256, D)
        d_cols = dot(d_head, pick_cols[...]).astype(BF16)
        grad = dot(text_t[at], d_cols).reshape(NZ, CHUNK, COLS)
        grad_head[:, pl.ds(0, CHUNK)] += grad

    dfeat_plane.ready(0)
    backward_block(blocks[0])
    dhead_plane.x2()
    dfeat_plane.y2()
    dfeat_plane.ready(1)
    backward_block(blocks[1])
    dhead_plane.y1()
    dfeat_plane.ready(2)
    backward_block(blocks[2])
    dfeat_plane.y3()
    dhead_plane.y2()
    dfeat_plane.ready(3)
    backward_block(blocks[3])

    def pack(at):
        for part in range(3):
            width = min(384, HIDDEN - 384 * part)
            lanes = pl.ds(384 * part, width)
            packed[at, pl.ds(OUT * part, OUT), pl.ds(0, width)] = grad_in[at, pl.ds(0, OUT), lanes]
            packed[at, pl.ds(OUT * (part + 3), OUT), pl.ds(0, width)] = grad_out[
                at, pl.ds(0, OUT), lanes
            ]

    class RingSum:
        def __init__(self, buf, rows, stage, land, far_up):
            self.buf, self.rows, self.stage, self.land = buf, rows, stage, land
            self.first = (1, 2) if far_up else (2, 1)
            self.copy = [None, None]

        def step(self, at):
            for way in range(2):
                if at < self.first[way]:
                    continue
                dest = (z + 5 - at) % 8 if way == 0 else (z + 3 + at) % 8
                term = self.buf[dest, self.rows]
                if at > self.first[way]:
                    self.copy[way].wait_recv()
                    term += self.land[way, at - 2, self.rows].astype(F32)
                self.stage[way, at - 1, self.rows] = term.astype(BF16)
                self.copy[way] = push(
                    self.stage.at[way, at - 1, self.rows],
                    self.land.at[way, at - 1, self.rows],
                    (z_up, z_down)[way],
                )

        def total(self):
            for way in range(2):
                self.copy[way].wait_recv()
            away = [self.land[way, 3, self.rows].astype(F32) for way in range(2)]
            return self.buf[z, self.rows] + away[0] + away[1]

    first, second = pl.ds(0, 64), pl.ds(64, 48)
    rings = (
        RingSum(packed, first, stage_main, land_main, True),
        RingSum(packed, second, stage_main, land_main, False),
    )
    ring_head = RingSum(grad_head, pl.ds(0, HEAD_CHUNK), stage_head, land_head, True)
    pack((z + 4) % 8)
    for ring in rings:
        ring.step(1)
    pack((z + 3) % 8)
    pack((z + 5) % 8)
    for ring in rings:
        ring.step(2)
    pack((z + 2) % 8)
    pack((z + 6) % 8)
    dhead_plane.y3()
    for ring in rings:
        ring.step(3)
    pack((z + 1) % 8)
    pack((z + 7) % 8)
    pack(z)
    for ring in rings:
        ring.step(4)
    for which in range(4):
        dhead_plane.ready(which)
        head_block(blocks[which])
    for at in range(1, 5):
        ring_head.step(at)
    for copy in loss_copies:
        copy.wait_recv()
    loss_out[...] = ((losses[0] + losses[1]) + (losses[2] + losses[3]))[:1]
    packed[z, first] = rings[0].total()
    packed[z, second] = rings[1].total()
    for part in range(3):
        width = min(384, HIDDEN - 384 * part)
        lanes = pl.ds(384 * part, width)
        in_out[:, lanes] = packed[z, pl.ds(OUT * part, OUT), pl.ds(0, width)]
        out_out[:, lanes] = packed[z, pl.ds(OUT * (part + 3), OUT), pl.ds(0, width)]
    head_out[...] = ring_head.total()[:OUT]
    links.drain()


def copy_out(*refs):
    for src, dst in zip(refs[:4], refs[4:]):
        dst[...] = src[...]


def on_device(
    images,
    captions,
    image_gain,
    fc_in,
    fc_out,
    text_gain,
    text_head,
    caption_ids,
    logit_scale,
    logit_bias,
):
    whole = pl.BlockSpec(memory_space=pltpu.VMEM)
    far = pl.BlockSpec(memory_space=pl.ANY)
    scalar = pl.BlockSpec(memory_space=pltpu.SMEM)
    vmem = pltpu.VMEM
    results = (
        jax.ShapeDtypeStruct((1, ROWS), F32),
        jax.ShapeDtypeStruct((OUT, HIDDEN), F32),
        jax.ShapeDtypeStruct((OUT, HIDDEN), F32),
        jax.ShapeDtypeStruct((OUT, COLS), F32),
    )
    found = pl.pallas_call(
        kernel,
        out_shape=results,
        in_specs=[far, far, whole, far, far, whole, far, whole, scalar, scalar],
        out_specs=(whole, whole, whole, whole),
        scratch_shapes=[
            vmem((HIDDEN, D), BF16),
            vmem((HIDDEN, D), BF16),
            vmem((COLS, D), BF16),
            vmem((4, QUARTER, D), BF16),
            vmem((4, QUARTER, D), BF16),
            vmem((32, QUARTER, D), BF16),
            vmem((32, QUARTER, D), BF16),
            vmem((32, QUARTER, D), BF16),
            vmem((32, QUARTER, D), BF16),
            vmem((4, QUARTER, D), F32),
            vmem((4, QUARTER, D), F32),
            vmem((4, QUARTER, D), F32),
            vmem((3, 2, QUARTER, D), F32),
            vmem((3, QUARTER, D), F32),
            vmem((3, QUARTER, D), F32),
            vmem((4, ROWS, COLS), BF16),
            vmem((4, QUARTER, D), F32),
            vmem((4, QUARTER, D), BF16),
            vmem((4, QUARTER, D), BF16),
            vmem((NZ, 2, QUARTER, D), BF16),
            vmem((NZ, 2, QUARTER, D), BF16),
            vmem((16, QUARTER, ROWS), F32),
            vmem((16, QUARTER, ROWS), F32),
            vmem((4, QUARTER, ROWS), F32),
            vmem((4, 8, ROWS), F32),
            vmem((NZ * CHUNK, D), BF16),
            vmem((D, COLS), BF16),
            vmem((4, 256, HIDDEN), BF16),
            vmem((4, 256, HIDDEN), F32),
            vmem((4, NZ * CHUNK, 256), BF16),
            vmem((4, NZ * CHUNK, 256), BF16),
            vmem((NZ, CHUNK, HIDDEN), F32),
            vmem((NZ, CHUNK, HIDDEN), F32),
            vmem((NZ, HEAD_CHUNK, COLS), F32),
            vmem((NZ, 112, 384), F32),
            vmem((2, 4, 112, 384), BF16),
            vmem((2, 4, HEAD_CHUNK, COLS), BF16),
            vmem((2, 4, 112, 384), BF16),
            vmem((2, 4, HEAD_CHUNK, COLS), BF16),
            pltpu.SemaphoreType.DMA((COPIES,)),
            pltpu.SemaphoreType.DMA((COPIES,)),
            pltpu.SemaphoreType.DMA((7,)),
        ],
        compiler_params=pltpu.CompilerParams(
            collective_id=0, has_side_effects=True, vmem_limit_bytes=56 * 1024 * 1024
        ),
        name="window",
    )(
        images.reshape(4, QUARTER, D),
        captions.reshape(4, QUARTER, D),
        image_gain,
        fc_in.T,
        fc_out,
        text_gain,
        text_head.T,
        caption_ids,
        logit_scale,
        logit_bias,
    )
    loss, grad_in, grad_out, grad_head = pl.pallas_call(
        copy_out,
        out_shape=results,
        in_specs=[whole] * 4,
        out_specs=(whole,) * 4,
        name="results",
    )(*found)
    return loss.reshape(ROWS), grad_in, grad_out.T, grad_head


def solution(mesh):
    placed = (
        P("dp", None),
        P("dp", None),
        P(),
        P(None, "mp"),
        P("mp", None),
        P(),
        P(None, "mp"),
        P("dp", None),
        P(),
        P(),
    )
    return jax.shard_map(
        on_device,
        mesh=mesh,
        in_specs=placed,
        out_specs=(P("dp"), P("dp", "mp"), P("mp", "dp"), P("dp", "mp")),
        check_vma=False,
    )
```

```python
import functools
import math

import jax
import jax.numpy as jnp
from jax import lax
from jax.experimental import pallas as pl
from jax.experimental.pallas import tpu as pltpu
from jax.sharding import PartitionSpec as P

NX, NY, NZ = 4, 4, 8
ROWS = 128
QUARTER = 32
D = 1152
HIDDEN = 1076
COLS = 288
OUT = 18
CHUNK = 24
HEAD_CHUNK = 32
COPIES = 200
F32, BF16 = jnp.float32, jnp.bfloat16
GELU = math.sqrt(2.0 / math.pi)


def dot(left, right):
    return jnp.dot(left, right, preferred_element_type=F32)


def dot_last(left, right):
    return lax.dot_general(left, right, (((1,), (1,)), ((), ())), preferred_element_type=F32)


def layer_norm(values, gain):
    center = values - jnp.mean(values, -1, keepdims=True)
    spread = jnp.mean(center * center, -1, keepdims=True)
    return (center * lax.rsqrt(spread + 1e-06) * gain).astype(BF16)


def unit_scale(values):
    return lax.rsqrt(jnp.sum(values * values, -1, keepdims=True) + 1e-06)


def unit_grad(values, scale, grad):
    inner = jnp.sum(values * grad, -1, keepdims=True)
    return scale * (grad - values * (scale * scale * inner))


def gelu_tanh(pre):
    return jnp.tanh(GELU * (pre + 0.044715 * pre * pre * pre))


def gelu(pre, bend):
    return (0.5 * pre * (1.0 + bend)).astype(BF16)


def gelu_slope(pre, bend):
    return 0.5 * (1.0 + bend) + 0.5 * pre * (1.0 - bend * bend) * (
        GELU * (1.0 + 3.0 * 0.044715 * pre * pre)
    )


def pair_terms(logit, sign, scale):
    arg = -sign * logit
    small = jnp.exp(-jnp.abs(arg))
    loss = jnp.maximum(arg, 0.0) + jnp.log1p(small)
    share = jnp.where(arg >= 0.0, 1.0, small) / (1.0 + small)
    return loss, -sign * share * scale


class Links:
    def __init__(self, send, recv):
        self.send, self.recv, self.started = send, recv, []

    def push(self, src, dst, device):
        at = len(self.started)
        copy = pltpu.make_async_remote_copy(
            src_ref=src,
            dst_ref=dst,
            send_sem=self.send.at[at],
            recv_sem=self.recv.at[at],
            device_id=device,
            device_id_type=pl.DeviceIdType.MESH,
        )
        copy.start()
        self.started.append(copy)
        return copy

    def drain(self):
        for copy in self.started:
            copy.wait_send()


def kernel(
    images,
    captions,
    image_gain,
    fc_in,
    fc_out,
    text_gain,
    text_head,
    ids,
    logit_scale,
    logit_bias,
    loss_out,
    in_out,
    out_out,
    head_out,
    w_in,
    w_out,
    w_head,
    own_images,
    own_captions,
    all_images,
    all_captions,
    all_dfeat,
    all_dhead,
    partial,
    d_img,
    d_txt,
    from_sibling,
    to_across,
    from_across,
    head_parts,
    head_full,
    txt_home,
    img_home,
    txt_units,
    img_units,
    sign_a,
    sign_b,
    matches,
    losses,
    pick_rows,
    pick_cols,
    act_all,
    slope_all,
    normed_t,
    text_t,
    grad_in,
    grad_out,
    grad_head,
    packed,
    stage_main,
    stage_head,
    land_main,
    land_head,
    send_sems,
    recv_sems,
    load_sems,
):
    dp, mp = lax.axis_index("dp"), lax.axis_index("mp")
    z, xh, y = dp // 8, (dp // 4) % 2, dp % 4
    xl, c = mp // 2, mp % 2
    x = 2 * xh + xl
    x_lo, x_pn = 2 * xh + (1 - xl), 3 - x
    y_above, y_below, y_far = (y + 1) % 4, (y + 3) % 4, (y + 2) % 4

    def place(z_, xh_, y_, xl_, c_):
        return {"dp": z_ * 8 + xh_ * 4 + y_, "mp": xl_ * 2 + c_}

    sibling = place(z, xh, y, xl, 1 - c)
    across = place(z, xh, y, 1 - xl, c)
    diagonal = place(z, xh, y, 1 - xl, 1 - c)
    partner = place(z, 1 - xh, y, 1 - xl, c)
    y_up, y_down = place(z, xh, y_above, xl, c), place(z, xh, y_below, xl, c)
    z_up, z_down = place((z + 1) % 8, xh, y, xl, c), place((z + 7) % 8, xh, y, xl, c)

    x_axis = dict(
        at=(x, x_lo, x_pn, 3 - x_lo), to=(across, partner), on=(partner, across)
    )
    y_axis = dict(
        at=(y, y_below, y_above, y_far), to=(y_up, y_down), on=(y_up, y_down)
    )

    def own_slot(half):
        return (y * 2 + c) * 4 + x if half == 0 else (x * 2 + c) * 4 + y

    pairs = [(images, own_images), (captions, own_captions)]
    for src, dst in ((images, all_images), (captions, all_captions)):
        for half in range(2):
            pairs.append((src.at[mp, pl.ds(16 * half, 16)], dst.at[half, own_slot(half)]))
    pairs.append((text_head, w_head))
    for src, dst in ((fc_in, w_in), (fc_out, w_out)):
        for part in range(3):
            lanes = pl.ds(384 * part, 384)
            pairs.append((src.at[:, lanes], dst.at[:, lanes]))
    loads = [
        pltpu.make_async_copy(src, dst, load_sems.at[at]) for at, (src, dst) in enumerate(pairs)
    ]
    for load in loads:
        load.start()

    barrier = pltpu.get_barrier_semaphore()
    peers = (sibling, across, diagonal, partner, y_up, y_down, z_up, z_down)
    for peer in peers:
        pl.semaphore_signal(barrier, inc=1, device_id=peer, device_id_type=pl.DeviceIdType.MESH)

    scale, bias = logit_scale[0], logit_bias[0]
    links = Links(send_sems, recv_sems)
    push = links.push
    pl.semaphore_wait(barrier, len(peers))

    class HalfGather:
        def __init__(self, buf, half, lead, follow):
            self.buf, self.half, self.lead, self.follow = buf, half, lead, follow

        def slot(self, which, lanes):
            at = (self.follow["at"][0] * 2 + c) * 4 + self.lead["at"][which]
            return self.buf.at[self.half, at, :, lanes]

        def group(self, which, part=None):
            first = (self.follow["at"][which] * 2 + c) * 4
            if part is None:
                return self.buf.at[self.half, pl.ds(first, 4)]
            return self.buf.at[self.half, pl.ds(first + 2 * part, 2)]

        def a1(self):
            own = self.slot(0, pl.ds(0, D))
            self.near = [push(own, own, self.lead["to"][way]) for way in range(2)]

        def a2(self):
            self.next = []
            for way in range(2):
                self.near[way].wait_recv()
                part = self.slot(1 + way, (pl.ds(0, 640), pl.ds(640, 512))[way])
                self.next.append(push(part, part, self.lead["on"][way]))

        def b1(self):
            for copy in self.next:
                copy.wait_recv()
            own = self.group(0)
            self.sib = [push(own, own, sibling)]
            self.near = [push(own, own, self.follow["to"][way]) for way in range(2)]

        def b2(self):
            self.next = []
            for way in range(2):
                self.near[way].wait_recv()
                part = self.group(1 + way, way)
                self.next.append(push(part, part, self.follow["on"][way]))
                whole = self.group(1 + way)
                self.sib.append(push(whole, whole, sibling))

        def b3(self):
            for copy in self.next:
                copy.wait_recv()
            whole = self.group(3)
            self.sib.append(push(whole, whole, sibling))

    class PlaneGather:
        def __init__(self, buf):
            self.buf = buf
            self.halves = (
                HalfGather(buf, 0, x_axis, y_axis),
                HalfGather(buf, 1, y_axis, x_axis),
            )

        def stage(self, name):
            for half in self.halves:
                getattr(half, name)()

        def block(self, which):
            rows = []
            for half in self.halves:
                half.sib[which].wait_recv()
                first = half.follow["at"][which] * 8
                rows.append(self.buf[half.half, pl.ds(first, 8)].reshape(128, D))
            return jnp.concatenate(rows, 0)

    class QuadSum:
        def __init__(self, buf, at):
            self.buf, self.at = buf, at

        def s1(self):
            self.first = [
                push(self.buf.at[1 - c], from_sibling.at[self.at, 0], sibling),
                push(self.buf.at[2 + 1 - c], from_sibling.at[self.at, 1], sibling),
            ]

        def s2(self):
            for copy in self.first:
                copy.wait_recv()
            away = self.buf[(1 - xl) * 2 + c] + from_sibling[self.at, 1 - xl]
            to_across[self.at] = away.astype(BF16)
            self.second = push(to_across.at[self.at], from_across.at[self.at], across)

        def total(self):
            mine = self.buf[mp] + from_sibling[self.at, xl]
            self.second.wait_recv()
            return mine + from_across[self.at].astype(F32)

    for load in loads[:6]:
        load.wait()
    images_plane, captions_plane = PlaneGather(all_images), PlaneGather(all_captions)
    images_plane.stage("a1")
    captions_plane.stage("a1")

    values = own_captions[...].reshape(ROWS, D).astype(F32)
    text_normed = layer_norm(values, text_gain[...].reshape(1, D))
    loads[6].wait()
    head_parts[mp] = dot_last(text_normed, w_head[...]).astype(BF16)
    head_copies = [
        push(head_parts.at[mp], head_parts.at[mp], peer) for peer in (sibling, across, diagonal)
    ]

    images_plane.stage("a2")
    captions_plane.stage("a2")

    values = own_images[...].reshape(ROWS, D).astype(F32)
    normed = layer_norm(values, image_gain[...].reshape(1, D))
    for load in loads[7:10]:
        load.wait()
    pre = dot_last(normed, w_in[...])
    act = gelu(pre, gelu_tanh(pre))
    for load in loads[10:]:
        load.wait()
    partial[...] = dot(act, w_out[...]).reshape(partial.shape)
    feat_sum = QuadSum(partial, 0)
    feat_sum.s1()
    images_plane.stage("b1")
    captions_plane.stage("b1")

    chunk = lax.broadcasted_iota(jnp.int32, (NZ, CHUNK, D), 0)
    inside = lax.broadcasted_iota(jnp.int32, (NZ, CHUNK, D), 1)
    col = lax.broadcasted_iota(jnp.int32, (NZ, CHUNK, D), 2)
    pos = xh * 4 + y
    picked = (col == chunk * (8 * OUT) + pos * OUT + inside) & (inside < OUT)
    pick_rows[...] = jnp.where(picked, 1.0, 0.0).reshape(NZ * CHUNK, D).astype(BF16)
    row = lax.broadcasted_iota(jnp.int32, (D, COLS), 0)
    col = lax.broadcasted_iota(jnp.int32, (D, COLS), 1)
    pick_cols[...] = jnp.where(row == mp * COLS + col, 1.0, 0.0).astype(BF16)

    caption = lax.broadcasted_iota(jnp.int32, (ROWS, ROWS), 0)
    match = jnp.where(caption == ids[...], 1.0, -1.0).astype(F32)
    sign_a[...] = jnp.full(sign_a.shape, -1.0, F32)
    sign_b[...] = jnp.full(sign_b.shape, -1.0, F32)
    matches[...] = match.reshape(matches.shape)
    sign_a[z * 2] = matches[mp]
    matches[...] = match.T.reshape(matches.shape)
    sign_b[z * 2] = matches[mp]
    grad_in[...] = jnp.zeros(grad_in.shape, F32)
    grad_out[...] = jnp.zeros(grad_out.shape, F32)
    grad_head[...] = jnp.zeros(grad_head.shape, F32)
    packed[...] = jnp.zeros(packed.shape, F32)

    feat_sum.s2()

    class UnitRing:
        def __init__(self, buf, col, share):
            self.buf, self.col, self.sharing, self.shared = buf, col, share, []

        def unit(self, z_, half=None):
            slot = self.buf.at[z_ % 8, self.col]
            return slot if half is None else slot.at[pl.ds(16 * half, 16)]

        def share(self, z_):
            if self.sharing:
                self.shared.append(push(self.unit(z_), self.buf.at[z_ % 8, 1], partner))

        def start(self):
            self.up = push(self.unit(z), self.unit(z), z_up)
            self.down = push(self.unit(z), self.unit(z), z_down)
            self.share(z)

        def step(self, at):
            half = at == 3
            self.up.wait_recv()
            unit = self.unit(z + 8 - at, 0 if half else None)
            self.up = push(unit, unit, z_up)
            self.share(z + 8 - at)
            self.down.wait_recv()
            unit = self.unit(z + at, 1 if half else None)
            self.down = push(unit, unit, z_down)
            self.share(z + at)

        def land(self):
            self.up.wait_recv()
            self.down.wait_recv()
            self.share(z + 4)

        def finish(self):
            for copy in self.shared:
                copy.wait_recv()

    for copy in head_copies:
        copy.wait_recv()
    head = jnp.concatenate([head_parts[part].astype(F32) for part in range(4)], 1)
    head_full[...] = head.reshape(head_full.shape)
    txt_home[...] = (head * unit_scale(head)).astype(BF16).reshape(txt_home.shape)
    txt_units[z, 0] = txt_home[mp]

    txt_partner = push(txt_units.at[z, 0], txt_units.at[z, 1], partner)
    txt_rings = (UnitRing(txt_units, 0, False), UnitRing(txt_units, 1, False))
    txt_rings[0].start()

    feat = own_images[mp].astype(F32) + feat_sum.total()
    feat_scale = unit_scale(feat)
    img_home[mp] = (feat * feat_scale).astype(BF16)
    img_units[z, 0] = img_home[mp]
    img_ring = UnitRing(img_units, 0, True)
    img_ring.start()
    img_copies = [push(img_home.at[mp], img_home.at[mp], peer) for peer in (sibling, across, diagonal)]

    txt_partner.wait_recv()
    txt_rings[1].start()

    def forward_block(which):
        values = images_plane.block(which).astype(F32)
        normed = layer_norm(values, image_gain[...].reshape(1, D))
        normed_t[which] = dot_last(pick_rows[...], normed).astype(BF16)
        pre = dot_last(normed, w_in[...])
        bend = gelu_tanh(pre)
        act_all[which] = gelu(pre, bend)
        slope_all[which] = gelu_slope(pre, bend)
        values = captions_plane.block(which).astype(F32)
        text_normed = layer_norm(values, text_gain[...].reshape(1, D))
        text_t[which] = dot_last(pick_rows[...], text_normed).astype(BF16)

    txt_rings[0].step(1)
    txt_rings[1].step(1)
    img_ring.step(1)
    images_plane.stage("b2")
    captions_plane.stage("b2")
    forward_block(0)
    txt_rings[0].step(2)
    txt_rings[1].step(2)
    img_ring.step(2)
    forward_block(1)
    txt_rings[0].step(3)
    txt_rings[1].step(3)
    img_ring.step(3)
    images_plane.stage("b3")
    captions_plane.stage("b3")
    forward_block(2)
    for copy in img_copies:
        copy.wait_recv()
    img_ring.land()
    for ring in txt_rings:
        ring.land()

    img_rows = img_home[...].reshape(ROWS, D)
    units = txt_units[...].reshape(16 * QUARTER, D)
    logit = scale * dot_last(units, img_rows) + bias
    loss, slope = pair_terms(logit, sign_a[...].reshape(16 * QUARTER, ROWS), scale)
    losses[mp] = jnp.broadcast_to(jnp.sum(loss, 0, keepdims=True), losses.shape[1:])
    loss_copies = [push(losses.at[mp], losses.at[mp], peer) for peer in (sibling, across, diagonal)]
    d_img[...] = dot(slope.T.astype(BF16), units).reshape(d_img.shape)
    img_sum = QuadSum(d_img, 1)
    img_sum.s1()
    img_ring.finish()
    txt_rows = txt_home[...].reshape(ROWS, D)
    units = img_units[...].reshape(16 * QUARTER, D)
    logit = scale * dot_last(units, txt_rows) + bias
    _, slope = pair_terms(logit, sign_b[...].reshape(16 * QUARTER, ROWS), scale)
    d_txt[...] = dot(slope.T.astype(BF16), units).reshape(d_txt.shape)
    txt_sum = QuadSum(d_txt, 2)
    txt_sum.s1()
    img_sum.s2()
    txt_sum.s2()
    forward_block(3)
    grad = unit_grad(feat, feat_scale, img_sum.total()).astype(BF16)
    for half in range(2):
        all_dfeat[half, own_slot(half)] = grad[16 * half : 16 * half + 16]
    dfeat_plane = PlaneGather(all_dfeat)
    dfeat_plane.stage("a1")
    head = head_full[mp]
    grad = unit_grad(head, unit_scale(head), txt_sum.total()).astype(BF16)
    for half in range(2):
        all_dhead[half, own_slot(half)] = grad[16 * half : 16 * half + 16]
    dhead_plane = PlaneGather(all_dhead)
    dhead_plane.stage("a1")

    def backward_block(which):
        d_feat = dfeat_plane.block(which)
        d_pre = (dot_last(d_feat, w_out[...]) * slope_all[which]).astype(BF16)
        d_feat_t = dot_last(pick_rows[...], d_feat).astype(BF16)
        grad_in[...] += dot(normed_t[which], d_pre).reshape(grad_in.shape)
        grad_out[...] += dot(d_feat_t, act_all[which]).reshape(grad_out.shape)

    def head_block(which):
        d_cols = dot(dhead_plane.block(which), pick_cols[...]).astype(BF16)
        grad = dot(text_t[which], d_cols).reshape(NZ, CHUNK, COLS)
        grad_head[:, pl.ds(0, CHUNK)] += grad

    dfeat_plane.stage("a2")
    dhead_plane.stage("a2")
    dfeat_plane.stage("b1")
    dhead_plane.stage("b1")
    backward_block(0)
    dfeat_plane.stage("b2")
    dhead_plane.stage("b2")
    backward_block(1)
    backward_block(2)
    dfeat_plane.stage("b3")
    dhead_plane.stage("b3")
    backward_block(3)

    def pack(at):
        for part in range(3):
            width = min(384, HIDDEN - 384 * part)
            lanes = pl.ds(384 * part, width)
            packed[at, pl.ds(OUT * part, OUT), pl.ds(0, width)] = grad_in[at, pl.ds(0, OUT), lanes]
            packed[at, pl.ds(OUT * (part + 3), OUT), pl.ds(0, width)] = grad_out[
                at, pl.ds(0, OUT), lanes
            ]

    class RingSum:
        def __init__(self, buf, rows, stage, land, far_up):
            self.buf, self.rows, self.stage, self.land = buf, rows, stage, land
            self.first = (1, 2) if far_up else (2, 1)
            self.copy = [None, None]

        def step(self, at):
            for way in range(2):
                if at < self.first[way]:
                    continue
                dest = (z + 5 - at) % 8 if way == 0 else (z + 3 + at) % 8
                term = self.buf[dest, self.rows]
                if at > self.first[way]:
                    self.copy[way].wait_recv()
                    term += self.land[way, at - 2, self.rows].astype(F32)
                self.stage[way, at - 1, self.rows] = term.astype(BF16)
                self.copy[way] = push(
                    self.stage.at[way, at - 1, self.rows],
                    self.land.at[way, at - 1, self.rows],
                    (z_up, z_down)[way],
                )

        def total(self):
            for way in range(2):
                self.copy[way].wait_recv()
            away = [self.land[way, 3, self.rows].astype(F32) for way in range(2)]
            return self.buf[z, self.rows] + away[0] + away[1]

    first, second = pl.ds(0, 64), pl.ds(64, 48)
    rings = (
        RingSum(packed, first, stage_main, land_main, True),
        RingSum(packed, second, stage_main, land_main, False),
    )
    ring_head = RingSum(grad_head, pl.ds(0, HEAD_CHUNK), stage_head, land_head, True)
    pack((z + 4) % 8)
    for ring in rings:
        ring.step(1)
    pack((z + 3) % 8)
    pack((z + 5) % 8)
    head_block(0)
    head_block(1)
    for ring in rings:
        ring.step(2)
    head_block(2)
    head_block(3)
    ring_head.step(1)
    pack((z + 2) % 8)
    pack((z + 6) % 8)
    for ring in rings:
        ring.step(3)
    pack((z + 1) % 8)
    pack((z + 7) % 8)
    pack(z)
    ring_head.step(2)
    for ring in rings:
        ring.step(4)
    ring_head.step(3)
    ring_head.step(4)
    for copy in loss_copies:
        copy.wait_recv()
    loss_out[...] = ((losses[0] + losses[1]) + (losses[2] + losses[3]))[:1]
    packed[z, first] = rings[0].total()
    packed[z, second] = rings[1].total()
    for part in range(3):
        width = min(384, HIDDEN - 384 * part)
        lanes = pl.ds(384 * part, width)
        in_out[:, lanes] = packed[z, pl.ds(OUT * part, OUT), pl.ds(0, width)]
        out_out[:, lanes] = packed[z, pl.ds(OUT * (part + 3), OUT), pl.ds(0, width)]
    head_out[...] = ring_head.total()[:OUT]
    links.drain()


def copy_out(*refs):
    for src, dst in zip(refs[:4], refs[4:]):
        dst[...] = src[...]


def on_device(
    images,
    captions,
    image_gain,
    fc_in,
    fc_out,
    text_gain,
    text_head,
    caption_ids,
    logit_scale,
    logit_bias,
):
    whole = pl.BlockSpec(memory_space=pltpu.VMEM)
    far = pl.BlockSpec(memory_space=pl.ANY)
    scalar = pl.BlockSpec(memory_space=pltpu.SMEM)
    vmem = pltpu.VMEM
    results = (
        jax.ShapeDtypeStruct((1, ROWS), F32),
        jax.ShapeDtypeStruct((OUT, HIDDEN), F32),
        jax.ShapeDtypeStruct((OUT, HIDDEN), F32),
        jax.ShapeDtypeStruct((OUT, COLS), F32),
    )
    found = pl.pallas_call(
        kernel,
        out_shape=results,
        in_specs=[far, far, whole, far, far, whole, far, whole, scalar, scalar],
        out_specs=(whole, whole, whole, whole),
        scratch_shapes=[
            vmem((HIDDEN, D), BF16),
            vmem((HIDDEN, D), BF16),
            vmem((COLS, D), BF16),
            vmem((4, QUARTER, D), BF16),
            vmem((4, QUARTER, D), BF16),
            vmem((2, 32, 16, D), BF16),
            vmem((2, 32, 16, D), BF16),
            vmem((2, 32, 16, D), BF16),
            vmem((2, 32, 16, D), BF16),
            vmem((4, QUARTER, D), F32),
            vmem((4, QUARTER, D), F32),
            vmem((4, QUARTER, D), F32),
            vmem((3, 2, QUARTER, D), F32),
            vmem((3, QUARTER, D), BF16),
            vmem((3, QUARTER, D), BF16),
            vmem((4, ROWS, COLS), BF16),
            vmem((4, QUARTER, D), F32),
            vmem((4, QUARTER, D), BF16),
            vmem((4, QUARTER, D), BF16),
            vmem((NZ, 2, QUARTER, D), BF16),
            vmem((NZ, 2, QUARTER, D), BF16),
            vmem((16, QUARTER, ROWS), F32),
            vmem((16, QUARTER, ROWS), F32),
            vmem((4, QUARTER, ROWS), F32),
            vmem((4, 8, ROWS), F32),
            vmem((NZ * CHUNK, D), BF16),
            vmem((D, COLS), BF16),
            vmem((4, 256, HIDDEN), BF16),
            vmem((4, 256, HIDDEN), F32),
            vmem((4, NZ * CHUNK, 256), BF16),
            vmem((4, NZ * CHUNK, 256), BF16),
            vmem((NZ, CHUNK, HIDDEN), F32),
            vmem((NZ, CHUNK, HIDDEN), F32),
            vmem((NZ, HEAD_CHUNK, COLS), F32),
            vmem((NZ, 112, 384), F32),
            vmem((2, 4, 112, 384), BF16),
            vmem((2, 4, HEAD_CHUNK, COLS), BF16),
            vmem((2, 4, 112, 384), BF16),
            vmem((2, 4, HEAD_CHUNK, COLS), BF16),
            pltpu.SemaphoreType.DMA((COPIES,)),
            pltpu.SemaphoreType.DMA((COPIES,)),
            pltpu.SemaphoreType.DMA((13,)),
        ],
        compiler_params=pltpu.CompilerParams(
            collective_id=0, has_side_effects=True, vmem_limit_bytes=56 * 1024 * 1024
        ),
        name="window",
    )(
        images.reshape(4, QUARTER, D),
        captions.reshape(4, QUARTER, D),
        image_gain,
        fc_in.T,
        fc_out,
        text_gain,
        text_head.T,
        caption_ids,
        logit_scale,
        logit_bias,
    )
    loss, grad_in, grad_out, grad_head = pl.pallas_call(
        copy_out,
        out_shape=results,
        in_specs=[whole] * 4,
        out_specs=(whole,) * 4,
        name="results",
    )(*found)
    return loss.reshape(ROWS), grad_in, grad_out.T, grad_head


def solution(mesh):
    placed = (
        P("dp", None),
        P("dp", None),
        P(),
        P(None, "mp"),
        P("mp", None),
        P(),
        P(None, "mp"),
        P("dp", None),
        P(),
        P(),
    )
    return jax.shard_map(
        on_device,
        mesh=mesh,
        in_specs=placed,
        out_specs=(P("dp"), P("dp", "mp"), P("mp", "dp"), P("dp", "mp")),
        check_vma=False,
    )
```

```python
import functools
import math

import jax
import jax.numpy as jnp
from jax import lax
from jax.experimental import pallas as pl
from jax.experimental.pallas import tpu as pltpu
from jax.sharding import PartitionSpec as P

NX, NY, NZ = 4, 4, 8
ROWS = 128
QUARTER = 32
D = 1152
HIDDEN = 1076
COLS = 288
OUT = 18
CHUNK = 24
HEAD_CHUNK = 32
COPIES = 200
F32, BF16 = jnp.float32, jnp.bfloat16
GELU = math.sqrt(2.0 / math.pi)


def dot(left, right):
    return jnp.dot(left, right, preferred_element_type=F32)


def dot_last(left, right):
    return lax.dot_general(left, right, (((1,), (1,)), ((), ())), preferred_element_type=F32)


def layer_norm(values, gain):
    center = values - jnp.mean(values, -1, keepdims=True)
    spread = jnp.mean(center * center, -1, keepdims=True)
    return (center * lax.rsqrt(spread + 1e-06) * gain).astype(BF16)


def unit_scale(values):
    return lax.rsqrt(jnp.sum(values * values, -1, keepdims=True) + 1e-06)


def unit_grad(values, scale, grad):
    inner = jnp.sum(values * grad, -1, keepdims=True)
    return scale * (grad - values * (scale * scale * inner))


def gelu_tanh(pre):
    return jnp.tanh(GELU * (pre + 0.044715 * pre * pre * pre))


def gelu(pre, bend):
    return (0.5 * pre * (1.0 + bend)).astype(BF16)


def gelu_slope(pre, bend):
    return 0.5 * (1.0 + bend) + 0.5 * pre * (1.0 - bend * bend) * (
        GELU * (1.0 + 3.0 * 0.044715 * pre * pre)
    )


def pair_terms(logit, sign, scale):
    arg = -sign * logit
    small = jnp.exp(-jnp.abs(arg))
    loss = jnp.maximum(arg, 0.0) + jnp.log1p(small)
    share = jnp.where(arg >= 0.0, 1.0, small) / (1.0 + small)
    return loss, -sign * share * scale


class Links:
    def __init__(self, send, recv):
        self.send, self.recv, self.started = send, recv, []

    def push(self, src, dst, device):
        at = len(self.started)
        copy = pltpu.make_async_remote_copy(
            src_ref=src,
            dst_ref=dst,
            send_sem=self.send.at[at],
            recv_sem=self.recv.at[at],
            device_id=device,
            device_id_type=pl.DeviceIdType.MESH,
        )
        copy.start()
        self.started.append(copy)
        return copy

    def drain(self):
        for copy in self.started:
            copy.wait_send()


def kernel(
    images,
    captions,
    image_gain,
    fc_in,
    fc_out,
    text_gain,
    text_head,
    ids,
    logit_scale,
    logit_bias,
    loss_out,
    in_out,
    out_out,
    head_out,
    w_in,
    w_out,
    w_head,
    own_images,
    own_captions,
    all_images,
    all_captions,
    all_dfeat,
    all_dhead,
    partial,
    d_img,
    d_txt,
    from_sibling,
    to_across,
    from_across,
    head_parts,
    head_full,
    txt_home,
    img_home,
    txt_units,
    img_units,
    sign_a,
    sign_b,
    matches,
    losses,
    pick_rows,
    pick_cols,
    act_all,
    slope_all,
    normed_t,
    grad_in,
    grad_out,
    grad_head,
    packed,
    stage_main,
    stage_head,
    land_main,
    land_head,
    send_sems,
    recv_sems,
    load_sems,
):
    dp, mp = lax.axis_index("dp"), lax.axis_index("mp")
    z, xh, y = dp // 8, (dp // 4) % 2, dp % 4
    xl, c = mp // 2, mp % 2
    x = 2 * xh + xl
    x_lo, x_pn = 2 * xh + (1 - xl), 3 - x
    y_above, y_below, y_far = (y + 1) % 4, (y + 3) % 4, (y + 2) % 4

    def place(z_, xh_, y_, xl_, c_):
        return {"dp": z_ * 8 + xh_ * 4 + y_, "mp": xl_ * 2 + c_}

    sibling = place(z, xh, y, xl, 1 - c)
    across = place(z, xh, y, 1 - xl, c)
    diagonal = place(z, xh, y, 1 - xl, 1 - c)
    partner = place(z, 1 - xh, y, 1 - xl, c)
    y_up, y_down = place(z, xh, y_above, xl, c), place(z, xh, y_below, xl, c)
    z_up, z_down = place((z + 1) % 8, xh, y, xl, c), place((z + 7) % 8, xh, y, xl, c)

    x_axis = dict(
        at=(x, x_lo, x_pn, 3 - x_lo), to=(across, partner), on=(partner, across)
    )
    y_axis = dict(
        at=(y, y_below, y_above, y_far), to=(y_up, y_down), on=(y_up, y_down)
    )

    def own_slot(half):
        return (y * 2 + c) * 4 + x if half == 0 else (x * 2 + c) * 4 + y

    pairs = [(images, own_images), (captions, own_captions)]
    for src, dst in ((images, all_images), (captions, all_captions)):
        for half in range(2):
            pairs.append((src.at[mp, pl.ds(16 * half, 16)], dst.at[half, own_slot(half)]))
    pairs.append((text_head, w_head))
    for src, dst in ((fc_in, w_in), (fc_out, w_out)):
        for part in range(3):
            lanes = pl.ds(384 * part, 384)
            pairs.append((src.at[:, lanes], dst.at[:, lanes]))
    loads = [
        pltpu.make_async_copy(src, dst, load_sems.at[at]) for at, (src, dst) in enumerate(pairs)
    ]
    for load in loads:
        load.start()

    barrier = pltpu.get_barrier_semaphore()
    rounds = [place((z + step) % 8, xh, y, xl, c) for step in range(1, NZ)]
    peers = [sibling, across, diagonal, partner, y_up, y_down] + rounds
    for peer in peers:
        pl.semaphore_signal(barrier, inc=1, device_id=peer, device_id_type=pl.DeviceIdType.MESH)

    scale, bias = logit_scale[0], logit_bias[0]
    links = Links(send_sems, recv_sems)
    push = links.push

    class HalfGather:
        def __init__(self, buf, half, lead, follow):
            self.buf, self.half, self.lead, self.follow = buf, half, lead, follow

        def slot(self, which, lanes):
            at = (self.follow["at"][0] * 2 + c) * 4 + self.lead["at"][which]
            return self.buf.at[self.half, at, :, lanes]

        def group(self, which, part=None):
            first = (self.follow["at"][which] * 2 + c) * 4
            if part is None:
                return self.buf.at[self.half, pl.ds(first, 4)]
            return self.buf.at[self.half, pl.ds(first + 2 * part, 2)]

        def a1(self):
            own = self.slot(0, pl.ds(0, D))
            self.near = [push(own, own, self.lead["to"][way]) for way in range(2)]

        def a2(self):
            self.next = []
            for way in range(2):
                self.near[way].wait_recv()
                part = self.slot(1 + way, (pl.ds(0, 640), pl.ds(640, 512))[way])
                self.next.append(push(part, part, self.lead["on"][way]))

        def b1(self):
            for copy in self.next:
                copy.wait_recv()
            own = self.group(0)
            self.sib = [push(own, own, sibling)]
            self.near = [push(own, own, self.follow["to"][way]) for way in range(2)]

        def b2(self):
            self.next = []
            for way in range(2):
                self.near[way].wait_recv()
                part = self.group(1 + way, way)
                self.next.append(push(part, part, self.follow["on"][way]))
                whole = self.group(1 + way)
                self.sib.append(push(whole, whole, sibling))

        def b3(self):
            for copy in self.next:
                copy.wait_recv()
            whole = self.group(3)
            self.sib.append(push(whole, whole, sibling))

    class PlaneGather:
        def __init__(self, buf):
            self.buf = buf
            self.halves = (
                HalfGather(buf, 0, x_axis, y_axis),
                HalfGather(buf, 1, y_axis, x_axis),
            )

        def stage(self, name):
            for half in self.halves:
                getattr(half, name)()

        def block(self, which):
            rows = []
            for half in self.halves:
                half.sib[which].wait_recv()
                first = half.follow["at"][which] * 8
                rows.append(self.buf[half.half, pl.ds(first, 8)].reshape(128, D))
            return jnp.concatenate(rows, 0)

    class QuadSum:
        def __init__(self, buf, at):
            self.buf, self.at = buf, at

        def s1(self):
            self.first = [
                push(self.buf.at[1 - c], from_sibling.at[self.at, 0], sibling),
                push(self.buf.at[2 + 1 - c], from_sibling.at[self.at, 1], sibling),
            ]

        def s2(self):
            for copy in self.first:
                copy.wait_recv()
            away = self.buf[(1 - xl) * 2 + c] + from_sibling[self.at, 1 - xl]
            to_across[self.at] = away.astype(BF16)
            self.second = push(to_across.at[self.at], from_across.at[self.at], across)

        def total(self):
            mine = self.buf[mp] + from_sibling[self.at, xl]
            self.second.wait_recv()
            return mine + from_across[self.at].astype(F32)

    images_plane, captions_plane = PlaneGather(all_images), PlaneGather(all_captions)
    for load in loads[:6]:
        load.wait()

    values = own_captions[...].reshape(ROWS, D).astype(F32)
    text_normed = layer_norm(values, text_gain[...].reshape(1, D))
    loads[6].wait()
    head_parts[mp] = dot_last(text_normed, w_head[...]).astype(BF16)
    pl.semaphore_wait(barrier, len(peers))
    images_plane.stage("a1")
    captions_plane.stage("a1")
    head_copies = [
        push(head_parts.at[mp], head_parts.at[mp], peer) for peer in (sibling, across, diagonal)
    ]

    values = own_images[...].reshape(ROWS, D).astype(F32)
    normed = layer_norm(values, image_gain[...].reshape(1, D))
    for load in loads[7:10]:
        load.wait()
    pre = dot_last(normed, w_in[...])
    act = gelu(pre, gelu_tanh(pre))
    for load in loads[10:]:
        load.wait()
    partial[...] = dot(act, w_out[...]).reshape(partial.shape)
    feat_sum = QuadSum(partial, 0)
    feat_sum.s1()
    images_plane.stage("a2")
    captions_plane.stage("a2")

    chunk = lax.broadcasted_iota(jnp.int32, (NZ, CHUNK, D), 0)
    inside = lax.broadcasted_iota(jnp.int32, (NZ, CHUNK, D), 1)
    col = lax.broadcasted_iota(jnp.int32, (NZ, CHUNK, D), 2)
    pos = xh * 4 + y
    picked = (col == chunk * (8 * OUT) + pos * OUT + inside) & (inside < OUT)
    pick_rows[...] = jnp.where(picked, 1.0, 0.0).reshape(NZ * CHUNK, D).astype(BF16)
    row = lax.broadcasted_iota(jnp.int32, (D, COLS), 0)
    col = lax.broadcasted_iota(jnp.int32, (D, COLS), 1)
    pick_cols[...] = jnp.where(row == mp * COLS + col, 1.0, 0.0).astype(BF16)

    caption = lax.broadcasted_iota(jnp.int32, (ROWS, ROWS), 0)
    match = jnp.where(caption == ids[...], 1.0, -1.0).astype(F32)
    sign_a[...] = jnp.full(sign_a.shape, -1.0, F32)
    sign_b[...] = jnp.full(sign_b.shape, -1.0, F32)
    matches[...] = match.reshape(matches.shape)
    sign_a[z * 2] = matches[mp]
    matches[...] = match.T.reshape(matches.shape)
    sign_b[z * 2] = matches[mp]
    grad_in[...] = jnp.zeros(grad_in.shape, F32)
    grad_out[...] = jnp.zeros(grad_out.shape, F32)
    grad_head[...] = jnp.zeros(grad_head.shape, F32)
    packed[...] = jnp.zeros(packed.shape, F32)

    feat_sum.s2()

    class UnitRing:
        def __init__(self, buf, col, share):
            self.buf, self.col, self.sharing, self.shared = buf, col, share, []

        def unit(self, z_, half=None):
            slot = self.buf.at[z_ % 8, self.col]
            return slot if half is None else slot.at[pl.ds(16 * half, 16)]

        def share(self, z_):
            if self.sharing:
                self.shared.append(push(self.unit(z_), self.buf.at[z_ % 8, 1], partner))

        def start(self):
            self.up = push(self.unit(z), self.unit(z), z_up)
            self.down = push(self.unit(z), self.unit(z), z_down)
            self.share(z)

        def step(self, at):
            half = at == 3
            self.up.wait_recv()
            unit = self.unit(z + 8 - at, 0 if half else None)
            self.up = push(unit, unit, z_up)
            self.share(z + 8 - at)
            self.down.wait_recv()
            unit = self.unit(z + at, 1 if half else None)
            self.down = push(unit, unit, z_down)
            self.share(z + at)

        def land(self):
            self.up.wait_recv()
            self.down.wait_recv()
            self.share(z + 4)

        def finish(self):
            for copy in self.shared:
                copy.wait_recv()

    for copy in head_copies:
        copy.wait_recv()
    head = jnp.concatenate([head_parts[part].astype(F32) for part in range(4)], 1)
    head_full[...] = head.reshape(head_full.shape)
    txt_home[...] = (head * unit_scale(head)).astype(BF16).reshape(txt_home.shape)
    txt_units[z, 0] = txt_home[mp]

    txt_partner = push(txt_units.at[z, 0], txt_units.at[z, 1], partner)
    txt_rings = (UnitRing(txt_units, 0, False), UnitRing(txt_units, 1, False))
    txt_rings[0].start()
    images_plane.stage("b1")
    captions_plane.stage("b1")

    feat = own_images[mp].astype(F32) + feat_sum.total()
    feat_scale = unit_scale(feat)
    img_home[mp] = (feat * feat_scale).astype(BF16)
    img_units[z, 0] = img_home[mp]
    img_ring = UnitRing(img_units, 0, True)
    img_ring.start()
    img_copies = [push(img_home.at[mp], img_home.at[mp], peer) for peer in (sibling, across, diagonal)]

    txt_partner.wait_recv()
    txt_rings[1].start()

    def forward_block(which):
        values = images_plane.block(which).astype(F32)
        normed = layer_norm(values, image_gain[...].reshape(1, D))
        normed_t[which] = dot_last(pick_rows[...], normed).astype(BF16)
        pre = dot_last(normed, w_in[...])
        bend = gelu_tanh(pre)
        act_all[which] = gelu(pre, bend)
        slope_all[which] = gelu_slope(pre, bend)

    txt_rings[0].step(1)
    txt_rings[1].step(1)
    img_ring.step(1)
    images_plane.stage("b2")
    txt_rings[0].step(2)
    txt_rings[1].step(2)
    img_ring.step(2)
    captions_plane.stage("b2")
    forward_block(0)
    txt_rings[0].step(3)
    txt_rings[1].step(3)
    img_ring.step(3)
    images_plane.stage("b3")
    forward_block(1)
    for copy in img_copies:
        copy.wait_recv()
    img_ring.land()
    for ring in txt_rings:
        ring.land()

    captions_plane.stage("b3")

    img_rows = img_home[...].reshape(ROWS, D)
    units = txt_units[...].reshape(16 * QUARTER, D)
    logit = scale * dot_last(units, img_rows) + bias
    loss, slope = pair_terms(logit, sign_a[...].reshape(16 * QUARTER, ROWS), scale)
    losses[mp] = jnp.broadcast_to(jnp.sum(loss, 0, keepdims=True), losses.shape[1:])
    loss_copies = [push(losses.at[mp], losses.at[mp], peer) for peer in (sibling, across, diagonal)]
    d_img[...] = dot(slope.T.astype(BF16), units).reshape(d_img.shape)
    img_sum = QuadSum(d_img, 1)
    img_sum.s1()
    img_sum.s2()
    forward_block(2)
    img_ring.finish()
    txt_rows = txt_home[...].reshape(ROWS, D)
    units = img_units[...].reshape(16 * QUARTER, D)
    logit = scale * dot_last(units, txt_rows) + bias
    _, slope = pair_terms(logit, sign_b[...].reshape(16 * QUARTER, ROWS), scale)
    d_txt[...] = dot(slope.T.astype(BF16), units).reshape(d_txt.shape)
    txt_sum = QuadSum(d_txt, 2)
    txt_sum.s1()
    grad = unit_grad(feat, feat_scale, img_sum.total()).astype(BF16)
    for half in range(2):
        all_dfeat[half, own_slot(half)] = grad[16 * half : 16 * half + 16]
    dfeat_plane = PlaneGather(all_dfeat)
    dfeat_plane.stage("a1")
    txt_sum.s2()
    forward_block(3)
    head = head_full[mp]
    grad = unit_grad(head, unit_scale(head), txt_sum.total()).astype(BF16)
    for half in range(2):
        all_dhead[half, own_slot(half)] = grad[16 * half : 16 * half + 16]
    dhead_plane = PlaneGather(all_dhead)
    dhead_plane.stage("a1")

    def backward_block(which):
        d_feat = dfeat_plane.block(which)
        d_pre = (dot_last(d_feat, w_out[...]) * slope_all[which]).astype(BF16)
        d_feat_t = dot_last(pick_rows[...], d_feat).astype(BF16)
        grad_in[...] += dot(normed_t[which], d_pre).reshape(grad_in.shape)
        grad_out[...] += dot(d_feat_t, act_all[which]).reshape(grad_out.shape)

    def head_block(which):
        values = captions_plane.block(which).astype(F32)
        text_normed = layer_norm(values, text_gain[...].reshape(1, D))
        text_t = dot_last(pick_rows[...], text_normed).astype(BF16)
        d_cols = dot(dhead_plane.block(which), pick_cols[...]).astype(BF16)
        grad = dot(text_t, d_cols).reshape(NZ, CHUNK, COLS)
        grad_head[:, pl.ds(0, CHUNK)] += grad

    dfeat_plane.stage("a2")
    dhead_plane.stage("a2")
    dfeat_plane.stage("b1")
    dhead_plane.stage("b1")
    backward_block(0)
    dfeat_plane.stage("b2")
    dhead_plane.stage("b2")
    backward_block(1)
    backward_block(2)
    dfeat_plane.stage("b3")
    dhead_plane.stage("b3")
    backward_block(3)

    def pack(at):
        for part in range(3):
            width = min(384, HIDDEN - 384 * part)
            lanes = pl.ds(384 * part, width)
            packed[at, pl.ds(OUT * part, OUT), pl.ds(0, width)] = grad_in[at, pl.ds(0, OUT), lanes]
            packed[at, pl.ds(OUT * (part + 3), OUT), pl.ds(0, width)] = grad_out[
                at, pl.ds(0, OUT), lanes
            ]

    class RingSum:
        def __init__(self, buf, rows, stage, land, far_up):
            self.buf, self.rows, self.stage, self.land = buf, rows, stage, land
            self.first = (1, 2) if far_up else (2, 1)
            self.copy = [None, None]

        def step(self, at):
            for way in range(2):
                if at < self.first[way]:
                    continue
                dest = (z + 5 - at) % 8 if way == 0 else (z + 3 + at) % 8
                term = self.buf[dest, self.rows]
                if at > self.first[way]:
                    self.copy[way].wait_recv()
                    term += self.land[way, at - 2, self.rows].astype(F32)
                self.stage[way, at - 1, self.rows] = term.astype(BF16)
                self.copy[way] = push(
                    self.stage.at[way, at - 1, self.rows],
                    self.land.at[way, at - 1, self.rows],
                    (z_up, z_down)[way],
                )

        def total(self):
            for way in range(2):
                self.copy[way].wait_recv()
            away = [self.land[way, 3, self.rows].astype(F32) for way in range(2)]
            return self.buf[z, self.rows] + away[0] + away[1]

    first, second = pl.ds(0, 64), pl.ds(64, 48)
    rings = (
        RingSum(packed, first, stage_main, land_main, True),
        RingSum(packed, second, stage_main, land_main, False),
    )
    pack((z + 4) % 8)
    for ring in rings:
        ring.step(1)
    pack((z + 3) % 8)
    pack((z + 5) % 8)
    head_block(0)
    head_block(1)
    for ring in rings:
        ring.step(2)
    head_block(2)
    head_block(3)
    head_sends = []
    for step in range(1, NZ):
        stage_head[step - 1] = grad_head[(z + step) % 8].astype(BF16)
        slot = (stage_head.at[step - 1], land_head.at[step - 1])
        head_sends.append(push(*slot, rounds[step - 1]))
    pack((z + 2) % 8)
    pack((z + 6) % 8)
    for ring in rings:
        ring.step(3)
    pack((z + 1) % 8)
    pack((z + 7) % 8)
    pack(z)
    for ring in rings:
        ring.step(4)
    for copy in loss_copies:
        copy.wait_recv()
    loss_out[...] = ((losses[0] + losses[1]) + (losses[2] + losses[3]))[:1]
    packed[z, first] = rings[0].total()
    packed[z, second] = rings[1].total()
    for part in range(3):
        width = min(384, HIDDEN - 384 * part)
        lanes = pl.ds(384 * part, width)
        in_out[:, lanes] = packed[z, pl.ds(OUT * part, OUT), pl.ds(0, width)]
        out_out[:, lanes] = packed[z, pl.ds(OUT * (part + 3), OUT), pl.ds(0, width)]
    total = grad_head[z]
    for step in range(1, NZ):
        head_sends[step - 1].wait_recv()
        total += land_head[step - 1].astype(F32)
    head_out[...] = total[:OUT]
    links.drain()


def copy_out(*refs):
    for src, dst in zip(refs[:4], refs[4:]):
        dst[...] = src[...]


def on_device(
    images,
    captions,
    image_gain,
    fc_in,
    fc_out,
    text_gain,
    text_head,
    caption_ids,
    logit_scale,
    logit_bias,
):
    whole = pl.BlockSpec(memory_space=pltpu.VMEM)
    far = pl.BlockSpec(memory_space=pl.ANY)
    scalar = pl.BlockSpec(memory_space=pltpu.SMEM)
    vmem = pltpu.VMEM
    results = (
        jax.ShapeDtypeStruct((1, ROWS), F32),
        jax.ShapeDtypeStruct((OUT, HIDDEN), F32),
        jax.ShapeDtypeStruct((OUT, HIDDEN), F32),
        jax.ShapeDtypeStruct((OUT, COLS), F32),
    )
    found = pl.pallas_call(
        kernel,
        out_shape=results,
        in_specs=[far, far, whole, far, far, whole, far, whole, scalar, scalar],
        out_specs=(whole, whole, whole, whole),
        scratch_shapes=[
            vmem((HIDDEN, D), BF16),
            vmem((HIDDEN, D), BF16),
            vmem((COLS, D), BF16),
            vmem((4, QUARTER, D), BF16),
            vmem((4, QUARTER, D), BF16),
            vmem((2, 32, 16, D), BF16),
            vmem((2, 32, 16, D), BF16),
            vmem((2, 32, 16, D), BF16),
            vmem((2, 32, 16, D), BF16),
            vmem((4, QUARTER, D), F32),
            vmem((4, QUARTER, D), F32),
            vmem((4, QUARTER, D), F32),
            vmem((3, 2, QUARTER, D), F32),
            vmem((3, QUARTER, D), BF16),
            vmem((3, QUARTER, D), BF16),
            vmem((4, ROWS, COLS), BF16),
            vmem((4, QUARTER, D), F32),
            vmem((4, QUARTER, D), BF16),
            vmem((4, QUARTER, D), BF16),
            vmem((NZ, 2, QUARTER, D), BF16),
            vmem((NZ, 2, QUARTER, D), BF16),
            vmem((16, QUARTER, ROWS), F32),
            vmem((16, QUARTER, ROWS), F32),
            vmem((4, QUARTER, ROWS), F32),
            vmem((4, 8, ROWS), F32),
            vmem((NZ * CHUNK, D), BF16),
            vmem((D, COLS), BF16),
            vmem((4, 256, HIDDEN), BF16),
            vmem((4, 256, HIDDEN), F32),
            vmem((4, NZ * CHUNK, 256), BF16),
            vmem((NZ, CHUNK, HIDDEN), F32),
            vmem((NZ, CHUNK, HIDDEN), F32),
            vmem((NZ, HEAD_CHUNK, COLS), F32),
            vmem((NZ, 112, 384), F32),
            vmem((2, 4, 112, 384), BF16),
            vmem((NZ - 1, HEAD_CHUNK, COLS), BF16),
            vmem((2, 4, 112, 384), BF16),
            vmem((NZ - 1, HEAD_CHUNK, COLS), BF16),
            pltpu.SemaphoreType.DMA((COPIES,)),
            pltpu.SemaphoreType.DMA((COPIES,)),
            pltpu.SemaphoreType.DMA((13,)),
        ],
        compiler_params=pltpu.CompilerParams(
            collective_id=0, has_side_effects=True, vmem_limit_bytes=56 * 1024 * 1024
        ),
        name="window",
    )(
        images.reshape(4, QUARTER, D),
        captions.reshape(4, QUARTER, D),
        image_gain,
        fc_in.T,
        fc_out,
        text_gain,
        text_head.T,
        caption_ids,
        logit_scale,
        logit_bias,
    )
    loss, grad_in, grad_out, grad_head = pl.pallas_call(
        copy_out,
        out_shape=results,
        in_specs=[whole] * 4,
        out_specs=(whole,) * 4,
        name="results",
    )(*found)
    return loss.reshape(ROWS), grad_in, grad_out.T, grad_head


def solution(mesh):
    placed = (
        P("dp", None),
        P("dp", None),
        P(),
        P(None, "mp"),
        P("mp", None),
        P(),
        P(None, "mp"),
        P("dp", None),
        P(),
        P(),
    )
    return jax.shard_map(
        on_device,
        mesh=mesh,
        in_specs=placed,
        out_specs=(P("dp"), P("dp", "mp"), P("mp", "dp"), P("dp", "mp")),
        check_vma=False,
    )
```

```python
import functools
import math

import jax
import jax.numpy as jnp
from jax import lax
from jax.experimental import pallas as pl
from jax.experimental.pallas import tpu as pltpu
from jax.sharding import PartitionSpec as P

NX, NY, NZ = 4, 4, 8
ROWS = 128
QUARTER = 32
D = 1152
HIDDEN = 1076
COLS = 288
OUT = 18
CHUNK = 24
HEAD_CHUNK = 32
COPIES = 200
F32, BF16 = jnp.float32, jnp.bfloat16
GELU = math.sqrt(2.0 / math.pi)


def dot(left, right):
    return jnp.dot(left, right, preferred_element_type=F32)


def dot_last(left, right):
    return lax.dot_general(left, right, (((1,), (1,)), ((), ())), preferred_element_type=F32)


def layer_norm(values, gain):
    center = values - jnp.mean(values, -1, keepdims=True)
    spread = jnp.mean(center * center, -1, keepdims=True)
    return (center * lax.rsqrt(spread + 1e-06) * gain).astype(BF16)


def unit_scale(values):
    return lax.rsqrt(jnp.sum(values * values, -1, keepdims=True) + 1e-06)


def unit_grad(values, scale, grad):
    inner = jnp.sum(values * grad, -1, keepdims=True)
    return scale * (grad - values * (scale * scale * inner))


def gelu_tanh(pre):
    return jnp.tanh(GELU * (pre + 0.044715 * pre * pre * pre))


def gelu(pre, bend):
    return (0.5 * pre * (1.0 + bend)).astype(BF16)


def gelu_slope(pre, bend):
    return 0.5 * (1.0 + bend) + 0.5 * pre * (1.0 - bend * bend) * (
        GELU * (1.0 + 3.0 * 0.044715 * pre * pre)
    )


def pair_terms(logit, sign, scale):
    arg = -sign * logit
    small = jnp.exp(-jnp.abs(arg))
    loss = jnp.maximum(arg, 0.0) + jnp.log1p(small)
    share = jnp.where(arg >= 0.0, 1.0, small) / (1.0 + small)
    return loss, -sign * share * scale


class Links:
    def __init__(self, send, recv):
        self.send, self.recv, self.started = send, recv, []

    def push(self, src, dst, device):
        at = len(self.started)
        copy = pltpu.make_async_remote_copy(
            src_ref=src,
            dst_ref=dst,
            send_sem=self.send.at[at],
            recv_sem=self.recv.at[at],
            device_id=device,
            device_id_type=pl.DeviceIdType.MESH,
        )
        copy.start()
        self.started.append(copy)
        return copy

    def drain(self):
        for copy in self.started:
            copy.wait_send()


def kernel(
    images,
    captions,
    image_gain,
    fc_in,
    fc_out,
    text_gain,
    text_head,
    ids,
    logit_scale,
    logit_bias,
    loss_out,
    in_out,
    out_out,
    head_out,
    w_in,
    w_out,
    w_head,
    own_images,
    own_captions,
    all_images,
    all_captions,
    all_dfeat,
    all_dhead,
    partial,
    d_img,
    d_txt,
    from_sibling,
    to_across,
    from_across,
    head_parts,
    head_full,
    txt_home,
    img_home,
    txt_units,
    img_units,
    sign_a,
    sign_b,
    matches,
    losses,
    pick_rows,
    pick_cols,
    act_all,
    slope_all,
    normed_t,
    text_t,
    grad_in,
    grad_out,
    grad_head,
    packed,
    stage_main,
    stage_head,
    land_main,
    land_head,
    send_sems,
    recv_sems,
    load_sems,
):
    dp, mp = lax.axis_index("dp"), lax.axis_index("mp")
    z, xh, y = dp // 8, (dp // 4) % 2, dp % 4
    xl, c = mp // 2, mp % 2
    x = 2 * xh + xl
    x_lo, x_pn = 2 * xh + (1 - xl), 3 - x
    y_above, y_below, y_far = (y + 1) % 4, (y + 3) % 4, (y + 2) % 4

    def place(z_, xh_, y_, xl_, c_):
        return {"dp": z_ * 8 + xh_ * 4 + y_, "mp": xl_ * 2 + c_}

    sibling = place(z, xh, y, xl, 1 - c)
    across = place(z, xh, y, 1 - xl, c)
    diagonal = place(z, xh, y, 1 - xl, 1 - c)
    partner = place(z, 1 - xh, y, 1 - xl, c)
    y_up, y_down = place(z, xh, y_above, xl, c), place(z, xh, y_below, xl, c)
    z_up, z_down = place((z + 1) % 8, xh, y, xl, c), place((z + 7) % 8, xh, y, xl, c)

    x_axis = dict(
        at=(x, x_lo, x_pn, 3 - x_lo), to=(across, partner), on=(partner, across)
    )
    y_axis = dict(
        at=(y, y_below, y_above, y_far), to=(y_up, y_down), on=(y_up, y_down)
    )

    def own_slot(half):
        return (y * 2 + c) * 4 + x if half == 0 else (x * 2 + c) * 4 + y

    pairs = [(images, own_images), (captions, own_captions)]
    for src, dst in ((images, all_images), (captions, all_captions)):
        for half in range(2):
            pairs.append((src.at[mp, pl.ds(16 * half, 16)], dst.at[half, own_slot(half)]))
    pairs.append((text_head, w_head))
    for src, dst in ((fc_in, w_in), (fc_out, w_out)):
        for part in range(3):
            lanes = pl.ds(384 * part, 384)
            pairs.append((src.at[:, lanes], dst.at[:, lanes]))
    loads = [
        pltpu.make_async_copy(src, dst, load_sems.at[at]) for at, (src, dst) in enumerate(pairs)
    ]
    for load in loads:
        load.start()

    barrier = pltpu.get_barrier_semaphore()
    rounds = [place((z + step) % 8, xh, y, xl, c) for step in range(1, NZ)]
    peers = [sibling, across, diagonal, partner, y_up, y_down] + rounds
    for peer in peers:
        pl.semaphore_signal(barrier, inc=1, device_id=peer, device_id_type=pl.DeviceIdType.MESH)

    scale, bias = logit_scale[0], logit_bias[0]
    links = Links(send_sems, recv_sems)
    push = links.push

    class HalfGather:
        def __init__(self, buf, half, lead, follow):
            self.buf, self.half, self.lead, self.follow = buf, half, lead, follow

        def slot(self, which, lanes):
            at = (self.follow["at"][0] * 2 + c) * 4 + self.lead["at"][which]
            return self.buf.at[self.half, at, :, lanes]

        def group(self, which, part=None):
            first = (self.follow["at"][which] * 2 + c) * 4
            if part is None:
                return self.buf.at[self.half, pl.ds(first, 4)]
            return self.buf.at[self.half, pl.ds(first + 2 * part, 2)]

        def a1(self):
            own = self.slot(0, pl.ds(0, D))
            self.near = [push(own, own, self.lead["to"][way]) for way in range(2)]

        def a2(self):
            self.next = []
            for way in range(2):
                self.near[way].wait_recv()
                part = self.slot(1 + way, (pl.ds(0, 640), pl.ds(640, 512))[way])
                self.next.append(push(part, part, self.lead["on"][way]))

        def b1(self):
            for copy in self.next:
                copy.wait_recv()
            own = self.group(0)
            self.sib = [push(own, own, sibling)]
            self.near = [push(own, own, self.follow["to"][way]) for way in range(2)]

        def b2(self):
            self.next = []
            for way in range(2):
                self.near[way].wait_recv()
                part = self.group(1 + way, way)
                self.next.append(push(part, part, self.follow["on"][way]))
                whole = self.group(1 + way)
                self.sib.append(push(whole, whole, sibling))

        def b3(self):
            for copy in self.next:
                copy.wait_recv()
            whole = self.group(3)
            self.sib.append(push(whole, whole, sibling))

    class PlaneGather:
        def __init__(self, buf):
            self.buf = buf
            self.halves = (
                HalfGather(buf, 0, x_axis, y_axis),
                HalfGather(buf, 1, y_axis, x_axis),
            )

        def stage(self, name):
            for half in self.halves:
                getattr(half, name)()

        def block(self, which):
            rows = []
            for half in self.halves:
                half.sib[which].wait_recv()
                first = half.follow["at"][which] * 8
                rows.append(self.buf[half.half, pl.ds(first, 8)].reshape(128, D))
            return jnp.concatenate(rows, 0)

    class QuadSum:
        def __init__(self, buf, at):
            self.buf, self.at = buf, at

        def s1(self):
            self.first = [
                push(self.buf.at[1 - c], from_sibling.at[self.at, 0], sibling),
                push(self.buf.at[2 + 1 - c], from_sibling.at[self.at, 1], sibling),
            ]

        def s2(self):
            for copy in self.first:
                copy.wait_recv()
            away = self.buf[(1 - xl) * 2 + c] + from_sibling[self.at, 1 - xl]
            to_across[self.at] = away.astype(BF16)
            self.second = push(to_across.at[self.at], from_across.at[self.at], across)

        def total(self):
            mine = self.buf[mp] + from_sibling[self.at, xl]
            self.second.wait_recv()
            return mine + from_across[self.at].astype(F32)

    images_plane, captions_plane = PlaneGather(all_images), PlaneGather(all_captions)
    for load in loads[:6]:
        load.wait()

    values = own_captions[...].reshape(ROWS, D).astype(F32)
    text_normed = layer_norm(values, text_gain[...].reshape(1, D))
    loads[6].wait()
    head_parts[mp] = dot_last(text_normed, w_head[...]).astype(BF16)
    pl.semaphore_wait(barrier, len(peers))
    images_plane.stage("a1")
    captions_plane.stage("a1")
    head_copies = [
        push(head_parts.at[mp], head_parts.at[mp], peer) for peer in (sibling, across, diagonal)
    ]

    values = own_images[...].reshape(ROWS, D).astype(F32)
    normed = layer_norm(values, image_gain[...].reshape(1, D))
    for load in loads[7:10]:
        load.wait()
    pre = dot_last(normed, w_in[...])
    act = gelu(pre, gelu_tanh(pre))
    for load in loads[10:]:
        load.wait()
    partial[...] = dot(act, w_out[...]).reshape(partial.shape)
    feat_sum = QuadSum(partial, 0)
    feat_sum.s1()
    images_plane.stage("a2")
    captions_plane.stage("a2")

    chunk = lax.broadcasted_iota(jnp.int32, (NZ, CHUNK, D), 0)
    inside = lax.broadcasted_iota(jnp.int32, (NZ, CHUNK, D), 1)
    col = lax.broadcasted_iota(jnp.int32, (NZ, CHUNK, D), 2)
    pos = xh * 4 + y
    picked = (col == chunk * (8 * OUT) + pos * OUT + inside) & (inside < OUT)
    pick_rows[...] = jnp.where(picked, 1.0, 0.0).reshape(NZ * CHUNK, D).astype(BF16)
    row = lax.broadcasted_iota(jnp.int32, (D, COLS), 0)
    col = lax.broadcasted_iota(jnp.int32, (D, COLS), 1)
    pick_cols[...] = jnp.where(row == mp * COLS + col, 1.0, 0.0).astype(BF16)

    caption = lax.broadcasted_iota(jnp.int32, (ROWS, ROWS), 0)
    match = jnp.where(caption == ids[...], 1.0, -1.0).astype(F32)
    sign_a[...] = jnp.full(sign_a.shape, -1.0, F32)
    sign_b[...] = jnp.full(sign_b.shape, -1.0, F32)
    matches[...] = match.reshape(matches.shape)
    sign_a[z * 2] = matches[mp]
    matches[...] = match.T.reshape(matches.shape)
    sign_b[z * 2] = matches[mp]
    grad_in[...] = jnp.zeros(grad_in.shape, F32)
    grad_out[...] = jnp.zeros(grad_out.shape, F32)
    grad_head[...] = jnp.zeros(grad_head.shape, F32)
    packed[...] = jnp.zeros(packed.shape, F32)

    feat_sum.s2()

    class UnitRing:
        def __init__(self, buf, col, share):
            self.buf, self.col, self.sharing, self.shared = buf, col, share, []

        def unit(self, z_, half=None):
            slot = self.buf.at[z_ % 8, self.col]
            return slot if half is None else slot.at[pl.ds(16 * half, 16)]

        def share(self, z_):
            if self.sharing:
                self.shared.append(push(self.unit(z_), self.buf.at[z_ % 8, 1], partner))

        def start(self):
            self.up = push(self.unit(z), self.unit(z), z_up)
            self.down = push(self.unit(z), self.unit(z), z_down)
            self.share(z)

        def step(self, at):
            half = at == 3
            self.up.wait_recv()
            unit = self.unit(z + 8 - at, 0 if half else None)
            self.up = push(unit, unit, z_up)
            self.share(z + 8 - at)
            self.down.wait_recv()
            unit = self.unit(z + at, 1 if half else None)
            self.down = push(unit, unit, z_down)
            self.share(z + at)

        def land(self):
            self.up.wait_recv()
            self.down.wait_recv()
            self.share(z + 4)

        def finish(self):
            for copy in self.shared:
                copy.wait_recv()

    for copy in head_copies:
        copy.wait_recv()
    head = jnp.concatenate([head_parts[part].astype(F32) for part in range(4)], 1)
    head_full[...] = head.reshape(head_full.shape)
    txt_home[...] = (head * unit_scale(head)).astype(BF16).reshape(txt_home.shape)
    txt_units[z, 0] = txt_home[mp]

    txt_partner = push(txt_units.at[z, 0], txt_units.at[z, 1], partner)
    txt_rings = (UnitRing(txt_units, 0, False), UnitRing(txt_units, 1, False))
    txt_rings[0].start()
    images_plane.stage("b1")
    captions_plane.stage("b1")

    feat = own_images[mp].astype(F32) + feat_sum.total()
    feat_scale = unit_scale(feat)
    img_home[mp] = (feat * feat_scale).astype(BF16)
    img_units[z, 0] = img_home[mp]
    img_ring = UnitRing(img_units, 0, True)
    img_ring.start()
    img_copies = [push(img_home.at[mp], img_home.at[mp], peer) for peer in (sibling, across, diagonal)]

    txt_partner.wait_recv()
    txt_rings[1].start()

    def forward_block(which):
        values = images_plane.block(which).astype(F32)
        normed = layer_norm(values, image_gain[...].reshape(1, D))
        normed_t[which] = dot_last(pick_rows[...], normed).astype(BF16)
        pre = dot_last(normed, w_in[...])
        bend = gelu_tanh(pre)
        act_all[which] = gelu(pre, bend)
        slope_all[which] = gelu_slope(pre, bend)

    txt_rings[0].step(1)
    txt_rings[1].step(1)
    img_ring.step(1)
    images_plane.stage("b2")
    txt_rings[0].step(2)
    txt_rings[1].step(2)
    img_ring.step(2)
    captions_plane.stage("b2")
    forward_block(0)
    txt_rings[0].step(3)
    txt_rings[1].step(3)
    img_ring.step(3)
    images_plane.stage("b3")
    forward_block(1)
    for copy in img_copies:
        copy.wait_recv()
    img_ring.land()
    for ring in txt_rings:
        ring.land()

    captions_plane.stage("b3")

    img_rows = img_home[...].reshape(ROWS, D)
    units = txt_units[...].reshape(16 * QUARTER, D)
    logit = scale * dot_last(units, img_rows) + bias
    loss, slope = pair_terms(logit, sign_a[...].reshape(16 * QUARTER, ROWS), scale)
    losses[mp] = jnp.broadcast_to(jnp.sum(loss, 0, keepdims=True), losses.shape[1:])
    loss_copies = [push(losses.at[mp], losses.at[mp], peer) for peer in (sibling, across, diagonal)]
    d_img[...] = dot(slope.T.astype(BF16), units).reshape(d_img.shape)
    img_sum = QuadSum(d_img, 1)
    img_sum.s1()
    img_sum.s2()
    forward_block(2)
    img_ring.finish()
    txt_rows = txt_home[...].reshape(ROWS, D)
    units = img_units[...].reshape(16 * QUARTER, D)
    logit = scale * dot_last(units, txt_rows) + bias
    _, slope = pair_terms(logit, sign_b[...].reshape(16 * QUARTER, ROWS), scale)
    d_txt[...] = dot(slope.T.astype(BF16), units).reshape(d_txt.shape)
    txt_sum = QuadSum(d_txt, 2)
    txt_sum.s1()
    grad = unit_grad(feat, feat_scale, img_sum.total()).astype(BF16)
    for half in range(2):
        all_dfeat[half, own_slot(half)] = grad[16 * half : 16 * half + 16]
    dfeat_plane = PlaneGather(all_dfeat)
    dfeat_plane.stage("a1")
    txt_sum.s2()
    forward_block(3)
    dfeat_plane.stage("a2")
    head = head_full[mp]
    grad = unit_grad(head, unit_scale(head), txt_sum.total()).astype(BF16)
    for half in range(2):
        all_dhead[half, own_slot(half)] = grad[16 * half : 16 * half + 16]
    dhead_plane = PlaneGather(all_dhead)
    dhead_plane.stage("a1")

    def backward_block(which):
        d_feat = dfeat_plane.block(which)
        d_pre = (dot_last(d_feat, w_out[...]) * slope_all[which]).astype(BF16)
        d_feat_t = dot_last(pick_rows[...], d_feat).astype(BF16)
        grad_in[...] += dot(normed_t[which], d_pre).reshape(grad_in.shape)
        grad_out[...] += dot(d_feat_t, act_all[which]).reshape(grad_out.shape)

    def text_block(which):
        values = captions_plane.block(which).astype(F32)
        text_normed = layer_norm(values, text_gain[...].reshape(1, D))
        text_t[which] = dot_last(pick_rows[...], text_normed).astype(BF16)

    def head_block(which):
        d_cols = dot(dhead_plane.block(which), pick_cols[...]).astype(BF16)
        grad = dot(text_t[which], d_cols).reshape(NZ, CHUNK, COLS)
        grad_head[:, pl.ds(0, CHUNK)] += grad

    dfeat_plane.stage("b1")
    dhead_plane.stage("a2")
    text_block(0)
    text_block(1)
    backward_block(0)
    dhead_plane.stage("b1")
    text_block(2)
    text_block(3)
    dfeat_plane.stage("b2")
    backward_block(1)
    backward_block(2)
    dhead_plane.stage("b2")
    dfeat_plane.stage("b3")
    backward_block(3)

    def pack(at):
        for part in range(3):
            width = min(384, HIDDEN - 384 * part)
            lanes = pl.ds(384 * part, width)
            packed[at, pl.ds(OUT * part, OUT), pl.ds(0, width)] = grad_in[at, pl.ds(0, OUT), lanes]
            packed[at, pl.ds(OUT * (part + 3), OUT), pl.ds(0, width)] = grad_out[
                at, pl.ds(0, OUT), lanes
            ]

    class RingSum:
        def __init__(self, buf, rows, stage, land, far_up):
            self.buf, self.rows, self.stage, self.land = buf, rows, stage, land
            self.first = (1, 2) if far_up else (2, 1)
            self.copy = [None, None]

        def step(self, at):
            for way in range(2):
                if at < self.first[way]:
                    continue
                dest = (z + 5 - at) % 8 if way == 0 else (z + 3 + at) % 8
                term = self.buf[dest, self.rows]
                if at > self.first[way]:
                    self.copy[way].wait_recv()
                    term += self.land[way, at - 2, self.rows].astype(F32)
                self.stage[way, at - 1, self.rows] = term.astype(BF16)
                self.copy[way] = push(
                    self.stage.at[way, at - 1, self.rows],
                    self.land.at[way, at - 1, self.rows],
                    (z_up, z_down)[way],
                )

        def total(self):
            for way in range(2):
                self.copy[way].wait_recv()
            away = [self.land[way, 3, self.rows].astype(F32) for way in range(2)]
            return self.buf[z, self.rows] + away[0] + away[1]

    first, second = pl.ds(0, 64), pl.ds(64, 48)
    rings = (
        RingSum(packed, first, stage_main, land_main, True),
        RingSum(packed, second, stage_main, land_main, False),
    )
    pack((z + 4) % 8)
    for ring in rings:
        ring.step(1)
    dhead_plane.stage("b3")
    pack((z + 3) % 8)
    pack((z + 5) % 8)
    head_block(0)
    head_block(1)
    for ring in rings:
        ring.step(2)
    head_block(2)
    head_block(3)
    head_sends = []
    for step in range(1, NZ):
        stage_head[step - 1] = grad_head[(z + step) % 8].astype(BF16)
        slot = (stage_head.at[step - 1], land_head.at[step - 1])
        head_sends.append(push(*slot, rounds[step - 1]))
    pack((z + 2) % 8)
    pack((z + 6) % 8)
    for ring in rings:
        ring.step(3)
    pack((z + 1) % 8)
    pack((z + 7) % 8)
    pack(z)
    for ring in rings:
        ring.step(4)
    for copy in loss_copies:
        copy.wait_recv()
    loss_out[...] = ((losses[0] + losses[1]) + (losses[2] + losses[3]))[:1]
    packed[z, first] = rings[0].total()
    packed[z, second] = rings[1].total()
    for part in range(3):
        width = min(384, HIDDEN - 384 * part)
        lanes = pl.ds(384 * part, width)
        in_out[:, lanes] = packed[z, pl.ds(OUT * part, OUT), pl.ds(0, width)]
        out_out[:, lanes] = packed[z, pl.ds(OUT * (part + 3), OUT), pl.ds(0, width)]
    total = grad_head[z]
    for step in range(1, NZ):
        head_sends[step - 1].wait_recv()
        total += land_head[step - 1].astype(F32)
    head_out[...] = total[:OUT]
    links.drain()


def copy_out(*refs):
    for src, dst in zip(refs[:4], refs[4:]):
        dst[...] = src[...]


def on_device(
    images,
    captions,
    image_gain,
    fc_in,
    fc_out,
    text_gain,
    text_head,
    caption_ids,
    logit_scale,
    logit_bias,
):
    whole = pl.BlockSpec(memory_space=pltpu.VMEM)
    far = pl.BlockSpec(memory_space=pl.ANY)
    scalar = pl.BlockSpec(memory_space=pltpu.SMEM)
    vmem = pltpu.VMEM
    results = (
        jax.ShapeDtypeStruct((1, ROWS), F32),
        jax.ShapeDtypeStruct((OUT, HIDDEN), F32),
        jax.ShapeDtypeStruct((OUT, HIDDEN), F32),
        jax.ShapeDtypeStruct((OUT, COLS), F32),
    )
    found = pl.pallas_call(
        kernel,
        out_shape=results,
        in_specs=[far, far, whole, far, far, whole, far, whole, scalar, scalar],
        out_specs=(whole, whole, whole, whole),
        scratch_shapes=[
            vmem((HIDDEN, D), BF16),
            vmem((HIDDEN, D), BF16),
            vmem((COLS, D), BF16),
            vmem((4, QUARTER, D), BF16),
            vmem((4, QUARTER, D), BF16),
            vmem((2, 32, 16, D), BF16),
            vmem((2, 32, 16, D), BF16),
            vmem((2, 32, 16, D), BF16),
            vmem((2, 32, 16, D), BF16),
            vmem((4, QUARTER, D), F32),
            vmem((4, QUARTER, D), F32),
            vmem((4, QUARTER, D), F32),
            vmem((3, 2, QUARTER, D), F32),
            vmem((3, QUARTER, D), BF16),
            vmem((3, QUARTER, D), BF16),
            vmem((4, ROWS, COLS), BF16),
            vmem((4, QUARTER, D), F32),
            vmem((4, QUARTER, D), BF16),
            vmem((4, QUARTER, D), BF16),
            vmem((NZ, 2, QUARTER, D), BF16),
            vmem((NZ, 2, QUARTER, D), BF16),
            vmem((16, QUARTER, ROWS), F32),
            vmem((16, QUARTER, ROWS), F32),
            vmem((4, QUARTER, ROWS), F32),
            vmem((4, 8, ROWS), F32),
            vmem((NZ * CHUNK, D), BF16),
            vmem((D, COLS), BF16),
            vmem((4, 256, HIDDEN), BF16),
            vmem((4, 256, HIDDEN), F32),
            vmem((4, NZ * CHUNK, 256), BF16),
            vmem((4, NZ * CHUNK, 256), BF16),
            vmem((NZ, CHUNK, HIDDEN), F32),
            vmem((NZ, CHUNK, HIDDEN), F32),
            vmem((NZ, HEAD_CHUNK, COLS), F32),
            vmem((NZ, 112, 384), F32),
            vmem((2, 4, 112, 384), BF16),
            vmem((NZ - 1, HEAD_CHUNK, COLS), BF16),
            vmem((2, 4, 112, 384), BF16),
            vmem((NZ - 1, HEAD_CHUNK, COLS), BF16),
            pltpu.SemaphoreType.DMA((COPIES,)),
            pltpu.SemaphoreType.DMA((COPIES,)),
            pltpu.SemaphoreType.DMA((13,)),
        ],
        compiler_params=pltpu.CompilerParams(
            collective_id=0, has_side_effects=True, vmem_limit_bytes=56 * 1024 * 1024
        ),
        name="window",
    )(
        images.reshape(4, QUARTER, D),
        captions.reshape(4, QUARTER, D),
        image_gain,
        fc_in.T,
        fc_out,
        text_gain,
        text_head.T,
        caption_ids,
        logit_scale,
        logit_bias,
    )
    loss, grad_in, grad_out, grad_head = pl.pallas_call(
        copy_out,
        out_shape=results,
        in_specs=[whole] * 4,
        out_specs=(whole,) * 4,
        name="results",
    )(*found)
    return loss.reshape(ROWS), grad_in, grad_out.T, grad_head


def solution(mesh):
    placed = (
        P("dp", None),
        P("dp", None),
        P(),
        P(None, "mp"),
        P("mp", None),
        P(),
        P(None, "mp"),
        P("dp", None),
        P(),
        P(),
    )
    return jax.shard_map(
        on_device,
        mesh=mesh,
        in_specs=placed,
        out_specs=(P("dp"), P("dp", "mp"), P("mp", "dp"), P("dp", "mp")),
        check_vma=False,
    )
```

```python
import functools
import math

import jax
import jax.numpy as jnp
from jax import lax
from jax.experimental import pallas as pl
from jax.experimental.pallas import tpu as pltpu
from jax.sharding import PartitionSpec as P

NX, NY, NZ = 4, 4, 8
ROWS = 128
QUARTER = 32
D = 1152
HIDDEN = 1076
COLS = 288
OUT = 18
CHUNK = 24
HEAD_CHUNK = 32
COPIES = 200
F32, BF16 = jnp.float32, jnp.bfloat16
GELU = math.sqrt(2.0 / math.pi)


def dot(left, right):
    return jnp.dot(left, right, preferred_element_type=F32)


def dot_last(left, right):
    return lax.dot_general(left, right, (((1,), (1,)), ((), ())), preferred_element_type=F32)


def layer_norm(values, gain):
    center = values - jnp.mean(values, -1, keepdims=True)
    spread = jnp.mean(center * center, -1, keepdims=True)
    return (center * lax.rsqrt(spread + 1e-06) * gain).astype(BF16)


def unit_scale(values):
    return lax.rsqrt(jnp.sum(values * values, -1, keepdims=True) + 1e-06)


def unit_grad(values, scale, grad):
    inner = jnp.sum(values * grad, -1, keepdims=True)
    return scale * (grad - values * (scale * scale * inner))


def gelu_tanh(pre):
    return jnp.tanh(GELU * (pre + 0.044715 * pre * pre * pre))


def gelu(pre, bend):
    return (0.5 * pre * (1.0 + bend)).astype(BF16)


def gelu_slope(pre, bend):
    return 0.5 * (1.0 + bend) + 0.5 * pre * (1.0 - bend * bend) * (
        GELU * (1.0 + 3.0 * 0.044715 * pre * pre)
    )


def pair_terms(logit, sign, scale):
    arg = -sign * logit
    small = jnp.exp(-jnp.abs(arg))
    loss = jnp.maximum(arg, 0.0) + jnp.log1p(small)
    share = jnp.where(arg >= 0.0, 1.0, small) / (1.0 + small)
    return loss, -sign * share * scale


class Links:
    def __init__(self, send, recv):
        self.send, self.recv, self.started = send, recv, []

    def push(self, src, dst, device):
        at = len(self.started)
        copy = pltpu.make_async_remote_copy(
            src_ref=src,
            dst_ref=dst,
            send_sem=self.send.at[at],
            recv_sem=self.recv.at[at],
            device_id=device,
            device_id_type=pl.DeviceIdType.MESH,
        )
        copy.start()
        self.started.append(copy)
        return copy

    def drain(self):
        for copy in self.started:
            copy.wait_send()


def kernel(
    images,
    captions,
    image_gain,
    fc_in,
    fc_out,
    text_gain,
    text_head,
    ids,
    logit_scale,
    logit_bias,
    loss_out,
    in_out,
    out_out,
    head_out,
    w_in,
    w_out,
    w_head,
    own_images,
    own_captions,
    all_images,
    all_captions,
    all_dfeat,
    all_dhead,
    partial,
    d_img,
    d_txt,
    from_sibling,
    to_across,
    from_across,
    head_parts,
    head_full,
    txt_home,
    img_home,
    txt_units,
    img_units,
    sign_a,
    sign_b,
    matches,
    losses,
    pick_rows,
    pick_cols,
    act_all,
    slope_all,
    normed_t,
    text_t,
    grad_in,
    grad_out,
    grad_head,
    packed,
    stage_main,
    stage_head,
    land_main,
    land_head,
    send_sems,
    recv_sems,
    load_sems,
):
    dp, mp = lax.axis_index("dp"), lax.axis_index("mp")
    z, xh, y = dp // 8, (dp // 4) % 2, dp % 4
    xl, c = mp // 2, mp % 2
    x = 2 * xh + xl
    x_lo, x_pn = 2 * xh + (1 - xl), 3 - x
    y_above, y_below, y_far = (y + 1) % 4, (y + 3) % 4, (y + 2) % 4

    def place(z_, xh_, y_, xl_, c_):
        return {"dp": z_ * 8 + xh_ * 4 + y_, "mp": xl_ * 2 + c_}

    sibling = place(z, xh, y, xl, 1 - c)
    across = place(z, xh, y, 1 - xl, c)
    diagonal = place(z, xh, y, 1 - xl, 1 - c)
    partner = place(z, 1 - xh, y, 1 - xl, c)
    y_up, y_down = place(z, xh, y_above, xl, c), place(z, xh, y_below, xl, c)
    z_up, z_down = place((z + 1) % 8, xh, y, xl, c), place((z + 7) % 8, xh, y, xl, c)

    x_axis = dict(
        at=(x, x_lo, x_pn, 3 - x_lo), to=(across, partner), on=(partner, across)
    )
    y_axis = dict(
        at=(y, y_below, y_above, y_far), to=(y_up, y_down), on=(y_up, y_down)
    )

    def own_slot(half):
        return (y * 2 + c) * 4 + x if half == 0 else (x * 2 + c) * 4 + y

    pairs = [(images, own_images), (captions, own_captions)]
    for src, dst in ((images, all_images), (captions, all_captions)):
        for half in range(2):
            pairs.append((src.at[mp, pl.ds(16 * half, 16)], dst.at[half, own_slot(half)]))
    pairs.append((text_head, w_head))
    for src, dst in ((fc_in, w_in), (fc_out, w_out)):
        for part in range(3):
            lanes = pl.ds(384 * part, 384)
            pairs.append((src.at[:, lanes], dst.at[:, lanes]))
    loads = [
        pltpu.make_async_copy(src, dst, load_sems.at[at]) for at, (src, dst) in enumerate(pairs)
    ]
    for load in loads:
        load.start()

    barrier = pltpu.get_barrier_semaphore()
    rounds = [place((z + step) % 8, xh, y, xl, c) for step in range(1, NZ)]
    peers = [sibling, across, diagonal, partner, y_up, y_down] + rounds
    for peer in peers:
        pl.semaphore_signal(barrier, inc=1, device_id=peer, device_id_type=pl.DeviceIdType.MESH)

    scale, bias = logit_scale[0], logit_bias[0]
    links = Links(send_sems, recv_sems)
    push = links.push

    class HalfGather:
        def __init__(self, buf, half, lead, follow):
            self.buf, self.half, self.lead, self.follow = buf, half, lead, follow

        def slot(self, which, lanes):
            at = (self.follow["at"][0] * 2 + c) * 4 + self.lead["at"][which]
            return self.buf.at[self.half, at, :, lanes]

        def group(self, which, part=None):
            first = (self.follow["at"][which] * 2 + c) * 4
            if part is None:
                return self.buf.at[self.half, pl.ds(first, 4)]
            return self.buf.at[self.half, pl.ds(first + 2 * part, 2)]

        def a1(self):
            own = self.slot(0, pl.ds(0, D))
            self.near = [push(own, own, self.lead["to"][way]) for way in range(2)]

        def a2(self):
            self.next = []
            for way in range(2):
                self.near[way].wait_recv()
                part = self.slot(1 + way, (pl.ds(0, 640), pl.ds(640, 512))[way])
                self.next.append(push(part, part, self.lead["on"][way]))

        def b1(self):
            for copy in self.next:
                copy.wait_recv()
            own = self.group(0)
            self.sib = [push(own, own, sibling)]
            self.near = [push(own, own, self.follow["to"][way]) for way in range(2)]

        def b2(self):
            self.next = []
            for way in range(2):
                self.near[way].wait_recv()
                part = self.group(1 + way, way)
                self.next.append(push(part, part, self.follow["on"][way]))
                whole = self.group(1 + way)
                self.sib.append(push(whole, whole, sibling))

        def b3(self):
            for copy in self.next:
                copy.wait_recv()
            whole = self.group(3)
            self.sib.append(push(whole, whole, sibling))

    class PlaneGather:
        def __init__(self, buf):
            self.buf = buf
            self.halves = (
                HalfGather(buf, 0, x_axis, y_axis),
                HalfGather(buf, 1, y_axis, x_axis),
            )

        def stage(self, name):
            for half in self.halves:
                getattr(half, name)()

        def block(self, which):
            rows = []
            for half in self.halves:
                half.sib[which].wait_recv()
                first = half.follow["at"][which] * 8
                rows.append(self.buf[half.half, pl.ds(first, 8)].reshape(128, D))
            return jnp.concatenate(rows, 0)

    class QuadSum:
        def __init__(self, buf, at):
            self.buf, self.at = buf, at

        def s1(self):
            self.first = [
                push(self.buf.at[1 - c], from_sibling.at[self.at, 0], sibling),
                push(self.buf.at[2 + 1 - c], from_sibling.at[self.at, 1], sibling),
            ]

        def s2(self):
            for copy in self.first:
                copy.wait_recv()
            away = self.buf[(1 - xl) * 2 + c] + from_sibling[self.at, 1 - xl]
            to_across[self.at] = away.astype(BF16)
            self.second = push(to_across.at[self.at], from_across.at[self.at], across)

        def total(self):
            mine = self.buf[mp] + from_sibling[self.at, xl]
            self.second.wait_recv()
            return mine + from_across[self.at].astype(F32)

    images_plane, captions_plane = PlaneGather(all_images), PlaneGather(all_captions)
    for load in loads[:6]:
        load.wait()

    values = own_captions[...].reshape(ROWS, D).astype(F32)
    text_normed = layer_norm(values, text_gain[...].reshape(1, D))
    loads[6].wait()
    head_parts[mp] = dot_last(text_normed, w_head[...]).astype(BF16)
    pl.semaphore_wait(barrier, len(peers))
    images_plane.stage("a1")
    captions_plane.stage("a1")
    head_copies = [
        push(head_parts.at[mp], head_parts.at[mp], peer) for peer in (sibling, across, diagonal)
    ]

    values = own_images[...].reshape(ROWS, D).astype(F32)
    normed = layer_norm(values, image_gain[...].reshape(1, D))
    for load in loads[7:10]:
        load.wait()
    pre = dot_last(normed, w_in[...])
    act = gelu(pre, gelu_tanh(pre))
    for load in loads[10:]:
        load.wait()
    partial[...] = dot(act, w_out[...]).reshape(partial.shape)
    feat_sum = QuadSum(partial, 0)
    feat_sum.s1()
    images_plane.stage("a2")
    captions_plane.stage("a2")

    chunk = lax.broadcasted_iota(jnp.int32, (NZ, CHUNK, D), 0)
    inside = lax.broadcasted_iota(jnp.int32, (NZ, CHUNK, D), 1)
    col = lax.broadcasted_iota(jnp.int32, (NZ, CHUNK, D), 2)
    pos = xh * 4 + y
    picked = (col == chunk * (8 * OUT) + pos * OUT + inside) & (inside < OUT)
    pick_rows[...] = jnp.where(picked, 1.0, 0.0).reshape(NZ * CHUNK, D).astype(BF16)
    row = lax.broadcasted_iota(jnp.int32, (D, COLS), 0)
    col = lax.broadcasted_iota(jnp.int32, (D, COLS), 1)
    pick_cols[...] = jnp.where(row == mp * COLS + col, 1.0, 0.0).astype(BF16)

    caption = lax.broadcasted_iota(jnp.int32, (ROWS, ROWS), 0)
    match = jnp.where(caption == ids[...], 1.0, -1.0).astype(F32)
    sign_a[...] = jnp.full(sign_a.shape, -1.0, F32)
    sign_b[...] = jnp.full(sign_b.shape, -1.0, F32)
    matches[...] = match.reshape(matches.shape)
    sign_a[z * 2] = matches[mp]
    matches[...] = match.T.reshape(matches.shape)
    sign_b[z * 2] = matches[mp]
    grad_in[...] = jnp.zeros(grad_in.shape, F32)
    grad_out[...] = jnp.zeros(grad_out.shape, F32)
    grad_head[...] = jnp.zeros(grad_head.shape, F32)
    packed[...] = jnp.zeros(packed.shape, F32)

    feat_sum.s2()

    class UnitRing:
        def __init__(self, buf, col, share):
            self.buf, self.col, self.sharing, self.shared = buf, col, share, []

        def unit(self, z_, half=None):
            slot = self.buf.at[z_ % 8, self.col]
            return slot if half is None else slot.at[pl.ds(16 * half, 16)]

        def share(self, z_):
            if self.sharing:
                self.shared.append(push(self.unit(z_), self.buf.at[z_ % 8, 1], partner))

        def start(self):
            self.up = push(self.unit(z), self.unit(z), z_up)
            self.down = push(self.unit(z), self.unit(z), z_down)
            self.share(z)

        def step(self, at):
            half = at == 3
            self.up.wait_recv()
            unit = self.unit(z + 8 - at, 0 if half else None)
            self.up = push(unit, unit, z_up)
            self.share(z + 8 - at)
            self.down.wait_recv()
            unit = self.unit(z + at, 1 if half else None)
            self.down = push(unit, unit, z_down)
            self.share(z + at)

        def land(self):
            self.up.wait_recv()
            self.down.wait_recv()
            self.share(z + 4)

        def finish(self):
            for copy in self.shared:
                copy.wait_recv()

    for copy in head_copies:
        copy.wait_recv()
    head = jnp.concatenate([head_parts[part].astype(F32) for part in range(4)], 1)
    head_full[...] = head.reshape(head_full.shape)
    txt_home[...] = (head * unit_scale(head)).astype(BF16).reshape(txt_home.shape)
    txt_units[z, 0] = txt_home[mp]

    txt_partner = push(txt_units.at[z, 0], txt_units.at[z, 1], partner)
    txt_rings = (UnitRing(txt_units, 0, False), UnitRing(txt_units, 1, False))
    txt_rings[0].start()
    images_plane.stage("b1")
    captions_plane.stage("b1")

    feat = own_images[mp].astype(F32) + feat_sum.total()
    feat_scale = unit_scale(feat)
    img_home[mp] = (feat * feat_scale).astype(BF16)
    img_units[z, 0] = img_home[mp]
    img_ring = UnitRing(img_units, 0, True)
    img_ring.start()
    img_copies = [push(img_home.at[mp], img_home.at[mp], peer) for peer in (sibling, across, diagonal)]

    txt_partner.wait_recv()
    txt_rings[1].start()

    def forward_block(which):
        values = images_plane.block(which).astype(F32)
        normed = layer_norm(values, image_gain[...].reshape(1, D))
        normed_t[which] = dot_last(pick_rows[...], normed).astype(BF16)
        pre = dot_last(normed, w_in[...])
        bend = gelu_tanh(pre)
        act_all[which] = gelu(pre, bend)
        slope_all[which] = gelu_slope(pre, bend)

    txt_rings[0].step(1)
    txt_rings[1].step(1)
    img_ring.step(1)
    images_plane.stage("b2")
    txt_rings[0].step(2)
    txt_rings[1].step(2)
    img_ring.step(2)
    txt_rings[0].step(3)
    txt_rings[1].step(3)
    img_ring.step(3)
    images_plane.stage("b3")
    forward_block(0)
    forward_block(1)
    for copy in img_copies:
        copy.wait_recv()
    img_ring.land()
    for ring in txt_rings:
        ring.land()

    img_rows = img_home[...].reshape(ROWS, D)
    units = txt_units[...].reshape(16 * QUARTER, D)
    logit = scale * dot_last(units, img_rows) + bias
    loss, slope = pair_terms(logit, sign_a[...].reshape(16 * QUARTER, ROWS), scale)
    losses[mp] = jnp.broadcast_to(jnp.sum(loss, 0, keepdims=True), losses.shape[1:])
    loss_copies = [push(losses.at[mp], losses.at[mp], peer) for peer in (sibling, across, diagonal)]
    d_img[...] = dot(slope.T.astype(BF16), units).reshape(d_img.shape)
    img_sum = QuadSum(d_img, 1)
    img_sum.s1()
    img_sum.s2()
    captions_plane.stage("b2")
    forward_block(2)
    img_ring.finish()
    txt_rows = txt_home[...].reshape(ROWS, D)
    units = img_units[...].reshape(16 * QUARTER, D)
    logit = scale * dot_last(units, txt_rows) + bias
    _, slope = pair_terms(logit, sign_b[...].reshape(16 * QUARTER, ROWS), scale)
    d_txt[...] = dot(slope.T.astype(BF16), units).reshape(d_txt.shape)
    txt_sum = QuadSum(d_txt, 2)
    txt_sum.s1()
    grad = unit_grad(feat, feat_scale, img_sum.total()).astype(BF16)
    for half in range(2):
        all_dfeat[half, own_slot(half)] = grad[16 * half : 16 * half + 16]
    dfeat_plane = PlaneGather(all_dfeat)
    dfeat_plane.stage("a1")
    txt_sum.s2()
    captions_plane.stage("b3")
    forward_block(3)
    dfeat_plane.stage("a2")
    head = head_full[mp]
    grad = unit_grad(head, unit_scale(head), txt_sum.total()).astype(BF16)
    for half in range(2):
        all_dhead[half, own_slot(half)] = grad[16 * half : 16 * half + 16]
    dhead_plane = PlaneGather(all_dhead)
    dhead_plane.stage("a1")

    def backward_block(which):
        d_feat = dfeat_plane.block(which)
        d_pre = (dot_last(d_feat, w_out[...]) * slope_all[which]).astype(BF16)
        d_feat_t = dot_last(pick_rows[...], d_feat).astype(BF16)
        grad_in[...] += dot(normed_t[which], d_pre).reshape(grad_in.shape)
        grad_out[...] += dot(d_feat_t, act_all[which]).reshape(grad_out.shape)

    def text_block(which):
        values = captions_plane.block(which).astype(F32)
        text_normed = layer_norm(values, text_gain[...].reshape(1, D))
        text_t[which] = dot_last(pick_rows[...], text_normed).astype(BF16)

    def head_block(which):
        d_cols = dot(dhead_plane.block(which), pick_cols[...]).astype(BF16)
        grad = dot(text_t[which], d_cols).reshape(NZ, CHUNK, COLS)
        grad_head[:, pl.ds(0, CHUNK)] += grad

    dfeat_plane.stage("b1")
    dhead_plane.stage("a2")
    text_block(0)
    text_block(1)
    backward_block(0)
    dhead_plane.stage("b1")
    text_block(2)
    text_block(3)
    dfeat_plane.stage("b2")
    backward_block(1)
    backward_block(2)
    dhead_plane.stage("b2")
    dfeat_plane.stage("b3")
    backward_block(3)

    def pack(at):
        for part in range(3):
            width = min(384, HIDDEN - 384 * part)
            lanes = pl.ds(384 * part, width)
            packed[at, pl.ds(OUT * part, OUT), pl.ds(0, width)] = grad_in[at, pl.ds(0, OUT), lanes]
            packed[at, pl.ds(OUT * (part + 3), OUT), pl.ds(0, width)] = grad_out[
                at, pl.ds(0, OUT), lanes
            ]

    class RingSum:
        def __init__(self, buf, rows, stage, land, far_up):
            self.buf, self.rows, self.stage, self.land = buf, rows, stage, land
            self.first = (1, 2) if far_up else (2, 1)
            self.copy = [None, None]

        def step(self, at):
            for way in range(2):
                if at < self.first[way]:
                    continue
                dest = (z + 5 - at) % 8 if way == 0 else (z + 3 + at) % 8
                term = self.buf[dest, self.rows]
                if at > self.first[way]:
                    self.copy[way].wait_recv()
                    term += self.land[way, at - 2, self.rows].astype(F32)
                self.stage[way, at - 1, self.rows] = term.astype(BF16)
                self.copy[way] = push(
                    self.stage.at[way, at - 1, self.rows],
                    self.land.at[way, at - 1, self.rows],
                    (z_up, z_down)[way],
                )

        def total(self):
            for way in range(2):
                self.copy[way].wait_recv()
            away = [self.land[way, 3, self.rows].astype(F32) for way in range(2)]
            return self.buf[z, self.rows] + away[0] + away[1]

    first, second = pl.ds(0, 64), pl.ds(64, 48)
    rings = (
        RingSum(packed, first, stage_main, land_main, True),
        RingSum(packed, second, stage_main, land_main, False),
    )
    pack((z + 4) % 8)
    for ring in rings:
        ring.step(1)
    dhead_plane.stage("b3")
    pack((z + 3) % 8)
    pack((z + 5) % 8)
    head_block(0)
    head_block(1)
    for ring in rings:
        ring.step(2)
    head_block(2)
    head_block(3)
    head_sends = []
    for step in range(1, NZ):
        stage_head[step - 1] = grad_head[(z + step) % 8].astype(BF16)
        slot = (stage_head.at[step - 1], land_head.at[step - 1])
        head_sends.append(push(*slot, rounds[step - 1]))
    pack((z + 2) % 8)
    pack((z + 6) % 8)
    for ring in rings:
        ring.step(3)
    pack((z + 1) % 8)
    pack((z + 7) % 8)
    pack(z)
    for ring in rings:
        ring.step(4)
    for copy in loss_copies:
        copy.wait_recv()
    loss_out[...] = ((losses[0] + losses[1]) + (losses[2] + losses[3]))[:1]
    packed[z, first] = rings[0].total()
    packed[z, second] = rings[1].total()
    for part in range(3):
        width = min(384, HIDDEN - 384 * part)
        lanes = pl.ds(384 * part, width)
        in_out[:, lanes] = packed[z, pl.ds(OUT * part, OUT), pl.ds(0, width)]
        out_out[:, lanes] = packed[z, pl.ds(OUT * (part + 3), OUT), pl.ds(0, width)]
    total = grad_head[z]
    for step in range(1, NZ):
        head_sends[step - 1].wait_recv()
        total += land_head[step - 1].astype(F32)
    head_out[...] = total[:OUT]
    links.drain()


def copy_out(*refs):
    for src, dst in zip(refs[:4], refs[4:]):
        dst[...] = src[...]


def on_device(
    images,
    captions,
    image_gain,
    fc_in,
    fc_out,
    text_gain,
    text_head,
    caption_ids,
    logit_scale,
    logit_bias,
):
    whole = pl.BlockSpec(memory_space=pltpu.VMEM)
    far = pl.BlockSpec(memory_space=pl.ANY)
    scalar = pl.BlockSpec(memory_space=pltpu.SMEM)
    vmem = pltpu.VMEM
    results = (
        jax.ShapeDtypeStruct((1, ROWS), F32),
        jax.ShapeDtypeStruct((OUT, HIDDEN), F32),
        jax.ShapeDtypeStruct((OUT, HIDDEN), F32),
        jax.ShapeDtypeStruct((OUT, COLS), F32),
    )
    found = pl.pallas_call(
        kernel,
        out_shape=results,
        in_specs=[far, far, whole, far, far, whole, far, whole, scalar, scalar],
        out_specs=(whole, whole, whole, whole),
        scratch_shapes=[
            vmem((HIDDEN, D), BF16),
            vmem((HIDDEN, D), BF16),
            vmem((COLS, D), BF16),
            vmem((4, QUARTER, D), BF16),
            vmem((4, QUARTER, D), BF16),
            vmem((2, 32, 16, D), BF16),
            vmem((2, 32, 16, D), BF16),
            vmem((2, 32, 16, D), BF16),
            vmem((2, 32, 16, D), BF16),
            vmem((4, QUARTER, D), F32),
            vmem((4, QUARTER, D), F32),
            vmem((4, QUARTER, D), F32),
            vmem((3, 2, QUARTER, D), F32),
            vmem((3, QUARTER, D), BF16),
            vmem((3, QUARTER, D), BF16),
            vmem((4, ROWS, COLS), BF16),
            vmem((4, QUARTER, D), F32),
            vmem((4, QUARTER, D), BF16),
            vmem((4, QUARTER, D), BF16),
            vmem((NZ, 2, QUARTER, D), BF16),
            vmem((NZ, 2, QUARTER, D), BF16),
            vmem((16, QUARTER, ROWS), F32),
            vmem((16, QUARTER, ROWS), F32),
            vmem((4, QUARTER, ROWS), F32),
            vmem((4, 8, ROWS), F32),
            vmem((NZ * CHUNK, D), BF16),
            vmem((D, COLS), BF16),
            vmem((4, 256, HIDDEN), BF16),
            vmem((4, 256, HIDDEN), F32),
            vmem((4, NZ * CHUNK, 256), BF16),
            vmem((4, NZ * CHUNK, 256), BF16),
            vmem((NZ, CHUNK, HIDDEN), F32),
            vmem((NZ, CHUNK, HIDDEN), F32),
            vmem((NZ, HEAD_CHUNK, COLS), F32),
            vmem((NZ, 112, 384), F32),
            vmem((2, 4, 112, 384), BF16),
            vmem((NZ - 1, HEAD_CHUNK, COLS), BF16),
            vmem((2, 4, 112, 384), BF16),
            vmem((NZ - 1, HEAD_CHUNK, COLS), BF16),
            pltpu.SemaphoreType.DMA((COPIES,)),
            pltpu.SemaphoreType.DMA((COPIES,)),
            pltpu.SemaphoreType.DMA((13,)),
        ],
        compiler_params=pltpu.CompilerParams(
            collective_id=0, has_side_effects=True, vmem_limit_bytes=56 * 1024 * 1024
        ),
        name="window",
    )(
        images.reshape(4, QUARTER, D),
        captions.reshape(4, QUARTER, D),
        image_gain,
        fc_in.T,
        fc_out,
        text_gain,
        text_head.T,
        caption_ids,
        logit_scale,
        logit_bias,
    )
    loss, grad_in, grad_out, grad_head = pl.pallas_call(
        copy_out,
        out_shape=results,
        in_specs=[whole] * 4,
        out_specs=(whole,) * 4,
        name="results",
    )(*found)
    return loss.reshape(ROWS), grad_in, grad_out.T, grad_head


def solution(mesh):
    placed = (
        P("dp", None),
        P("dp", None),
        P(),
        P(None, "mp"),
        P("mp", None),
        P(),
        P(None, "mp"),
        P("dp", None),
        P(),
        P(),
    )
    return jax.shard_map(
        on_device,
        mesh=mesh,
        in_specs=placed,
        out_specs=(P("dp"), P("dp", "mp"), P("mp", "dp"), P("dp", "mp")),
        check_vma=False,
    )
```
